256 devices in a mesh: ta: 64 (over z, y, x_hi), sa: 4 (over x_lo, core).
Axes of the slice: x: 4 (x_hi: 2, x_lo: 2; x = x_hi * 2 + x_lo), y: 4, z: 8, core: 2. Of those that a mesh axis runs over, the one named last changes fastest.
Arguments:
- even_modes: bfloat16 [16, 2, 4, 3, 64, 16, 128], P(None, None, None, None, 'ta', 'sa'), may hold values from -6 to 6
- hop_links: bfloat16 [2, 4, 2, 3, 3, 64, 16, 128], P(None, None, None, None, None, 'ta', 'sa'), may hold values from -3.5 to 3.5
- clover_inverse: float32 [2, 2, 6, 6, 64, 16, 128], P(None, None, None, None, 'ta', 'sa'), may hold values from -0.2 to 1
- momenta: int32 [16, 3], replicated, may hold values from -2 to 2
- mode_weights: float32 [16], replicated, may hold values from 0.5 to 2
- separations: int32 [64, 16], P('ta'), may hold values from 1 to 63
Outputs:
- odd_modes: bfloat16 [16, 2, 4, 3, 64, 16, 128], P(None, None, None, None, 'ta', 'sa')
- correlator: float32 [64, 16], P('ta')
The draws below stay inside these ranges and needn't reach their ends.
All inputs are finite; a program needn't handle non-finite values.
Results may differ from the reference program's by a relative error of at most 0.0055.
Values may be sent and summed in bfloat16 or wider, within the bound.
A program may use at most 128 MiB of HBM per device.

```python
import math
import jax
import jax.numpy as jnp
from jax import lax

NMODE = 16
NMOM = 16
LS = 16
NT = 64
YX = 128
NSEP = 16


def draw_clover_inverse(key, part):
    key = jax.random.fold_in(key, 7)
    first, second, third = jax.random.split(key, 3)
    sites = (NT, LS, YX)
    diagonal = jax.random.uniform(first, (2, 6) + sites, jnp.float32, 0.5, 1.0)
    draw_real = jax.random.uniform(second, (2, 6, 6) + sites, jnp.float32, -0.2, 0.2)
    draw_imag = jax.random.uniform(third, (2, 6, 6) + sites, jnp.float32, -0.2, 0.2)
    herm_real = 0.5 * (draw_real + jnp.swapaxes(draw_real, 1, 2))
    herm_imag = 0.5 * (draw_imag - jnp.swapaxes(draw_imag, 1, 2))
    identity = jnp.eye(6, dtype=jnp.float32)[None, :, :, None, None, None]
    real_part = herm_real * (1.0 - identity) + identity * diagonal[:, :, None]
    return jnp.stack([real_part, herm_imag], axis=1)


def with_ends(entries, key, least, largest):
    longest = entries.shape.index(max(entries.shape))
    spots = []
    for shift in (0, 1):
        where = [jax.random.randint(jax.random.fold_in(key, axis), (), 0, length) for axis, length in enumerate(entries.shape)]
        where[longest] = (where[longest] + shift) % entries.shape[longest]
        spots.append(tuple(where))
    return entries.at[spots[0]].set(least).at[spots[1]].set(largest)


def block_scale(stream_key, shape, shards, least, largest):
    loudness = 1.0
    for position, parts in shards:
        heights = jax.random.uniform(jax.random.fold_in(jax.random.fold_in(stream_key, 6), position), (parts,), jnp.float32, least / len(shards), largest / len(shards))
        loudness = loudness * jnp.repeat(jnp.exp(heights), shape[position] // parts).reshape((-1,) + (1,) * (len(shape) - 1 - position))
    return loudness


def scatter_about(stream_key, dims, scale, reach, cuts=(), held_as=jnp.bfloat16):
    factor_of = block_scale(stream_key, dims, cuts, -0.22, 0.18) if cuts else 1.0
    entries = jax.random.normal(stream_key, dims, jnp.float32) * scale * factor_of
    return jnp.minimum(jnp.maximum(entries, -reach), reach).astype(held_as)


def setup_inputs(seed: int = 0) -> dict:
    key_list = jax.random.split(jax.random.key(seed), 7)
    return {
        "even_modes": scatter_about(key_list[0], (NMODE, 2, 4, 3, NT, LS, YX), 1.0, 6.0, ((4, 64), (5, 4))),
        "hop_links": scatter_about(key_list[1], (2, 4, 2, 3, 3, NT, LS, YX), 3 ** -0.5, 3.5, ((5, 64), (6, 4))),
        "clover_inverse": draw_clover_inverse(jax.random.fold_in(key_list[6], 71), 0),
        "momenta": with_ends(jax.random.randint(key_list[3], (NMOM, 3), -2, 3), jax.random.fold_in(key_list[3], 1), -2, 2).astype(jnp.int32),
        "mode_weights": jnp.clip(jnp.exp(jax.random.uniform(key_list[4], (NMODE,), jnp.float32, math.log(0.5), math.log(2.0))), 0.5, 2.0),
        "separations": with_ends(jax.random.randint(key_list[5], (NT, NSEP), 1, NT), jax.random.fold_in(key_list[5], 1), 1, NT - 1).astype(jnp.int32),
    }


hop_kappa = 0.125
gamma_source = ((3, 2, 1, 0), (3, 2, 1, 0), (2, 3, 0, 1), (2, 3, 0, 1))
gamma_factor = ((3, 3, 2, 2), (1, 0, 0, 1), (3, 2, 2, 3), (0, 0, 0, 0))


def times_factor(real_part, imag_part, factor_code):
    if factor_code == 0:
        return real_part, imag_part
    if factor_code == 1:
        return -real_part, -imag_part
    if factor_code == 2:
        return -imag_part, real_part
    return imag_part, -real_part


def apply_gamma(spinor, d):
    spin_rows = []
    for s in range(4):
        source_spin = gamma_source[d][s]
        a, b = times_factor(spinor[:, 0, source_spin], spinor[:, 1, source_spin], gamma_factor[d][s])
        spin_rows.append(jnp.stack([a, b], axis=1))
    return jnp.stack(spin_rows, axis=2)


def color_times(link_field, spinor, adjoint):
    link_real = link_field[0]
    link_imag = link_field[1]
    if adjoint:
        link_real = jnp.swapaxes(link_real, 0, 1)
        link_imag = -jnp.swapaxes(link_imag, 0, 1)
    spinor_real = spinor[:, 0][:, :, None]
    spinor_imag = spinor[:, 1][:, :, None]
    link_real = link_real[None, None]
    link_imag = link_imag[None, None]
    out_real = jnp.sum(link_real * spinor_real - link_imag * spinor_imag, axis=3)
    out_imag = jnp.sum(link_real * spinor_imag + link_imag * spinor_real, axis=3)
    return jnp.stack([out_real, out_imag], axis=1)


def wilson_hop(forward, backward, link_field):
    running = jnp.zeros(forward[0].shape, jnp.float32)
    for d in range(4):
        ahead = color_times(link_field[0, d], forward[d], False)
        behind = color_times(link_field[1, d], backward[d], True)
        running = running + ahead - apply_gamma(ahead, d) + behind + apply_gamma(behind, d)
    return running


def clover_apply(clover, spinor):
    shape = spinor.shape
    halves = spinor.reshape((shape[0], 2, 2, 6) + shape[4:])
    half_real = halves[:, 0][:, :, None]
    half_imag = halves[:, 1][:, :, None]
    clover_real = clover[:, 0][None]
    clover_imag = clover[:, 1][None]
    out_real = jnp.sum(clover_real * half_real - clover_imag * half_imag, axis=3)
    out_imag = jnp.sum(clover_real * half_imag + clover_imag * half_real, axis=3)
    return jnp.stack([out_real, out_imag], axis=1).reshape(shape)


def parity_grid(t_values, z_values):
    half_row = LS // 2
    y_place = jnp.arange(LS * half_row, dtype=jnp.int32) // half_row
    return (t_values[:, None, None] + z_values[None, :, None] + y_place[None, None, :] + 1) % 2 == 1


def x_neighbours(even_field, odd_shift):
    shape = even_field.shape
    grouped = even_field.reshape(shape[:-1] + (LS, LS // 2))
    ahead_rows = jnp.roll(grouped, -1, axis=-1).reshape(shape)
    behind_rows = jnp.roll(grouped, 1, axis=-1).reshape(shape)
    return jnp.where(odd_shift, ahead_rows, even_field), jnp.where(odd_shift, even_field, behind_rows)


def meson_block(even_part, odd_part, time_value, z_values, momenta):
    half_row = LS // 2
    column = jnp.arange(LS * half_row, dtype=jnp.int32)
    y_grid = jnp.broadcast_to((column // half_row)[None, :], (z_values.shape[0], LS * half_row))
    z_grid = jnp.broadcast_to(z_values[:, None], y_grid.shape)
    x_half = (column % half_row)[None, :]
    even_place = 2 * x_half + (time_value + z_grid + y_grid) % 2
    odd_place = 2 * x_half + (time_value + z_grid + y_grid + 1) % 2
    x_place = jnp.concatenate([even_place.reshape(-1), odd_place.reshape(-1)]).astype(jnp.int32)
    y_place = jnp.concatenate([y_grid.reshape(-1), y_grid.reshape(-1)]).astype(jnp.int32)
    z_place = jnp.concatenate([z_grid.reshape(-1), z_grid.reshape(-1)]).astype(jnp.int32)
    lead_shape = even_part.shape[:4]
    vectors = jnp.concatenate([even_part.reshape(lead_shape + (-1,)), odd_part.reshape(lead_shape + (-1,))], axis=-1)
    wave_number = (momenta[:, 0:1] * x_place[None, :] + momenta[:, 1:2] * y_place[None, :] + momenta[:, 2:3] * z_place[None, :]) % LS
    phase_angle = wave_number.astype(jnp.float32) * (2.0 * math.pi / LS)
    cosine = jnp.cos(phase_angle)[:, None, None, None, :]
    sine_part = jnp.sin(phase_angle)[:, None, None, None, :]
    mode_real = vectors[:, 0].astype(jnp.float32)[None]
    mode_imag = vectors[:, 1].astype(jnp.float32)[None]
    left_rows = jnp.stack([mode_real * cosine - mode_imag * sine_part, -(mode_real * sine_part + mode_imag * cosine)]).astype(jnp.bfloat16)
    right_cols = jnp.stack([apply_gamma(vectors, k) for k in range(4)])
    return jnp.einsum("rpiscx,kjqscx->rpikjq", left_rows.astype(jnp.float32), right_cols.astype(jnp.float32), precision=lax.Precision.HIGHEST)


def meson_layout(product):
    real_part = product[0, ..., 0] - product[1, ..., 1]
    imag_part = product[0, ..., 1] + product[1, ..., 0]
    return jnp.stack([real_part, imag_part]).transpose(0, 3, 1, 2, 4)


def reference(even_modes, hop_links, clover_inverse, momenta, mode_weights, separations):
    half_row = LS // 2
    t_values = jnp.arange(NT, dtype=jnp.int32)
    z_values = jnp.arange(LS, dtype=jnp.int32)
    even_field = even_modes.astype(jnp.float32)
    odd_shift = parity_grid(t_values, z_values)
    x_ahead, x_behind = x_neighbours(even_field, odd_shift)
    ahead_sign = jnp.where(t_values == NT - 1, -1.0, 1.0).astype(jnp.float32)[:, None, None]
    behind_sign = jnp.where(t_values == 0, -1.0, 1.0).astype(jnp.float32)[:, None, None]
    forward = (x_ahead, jnp.roll(even_field, -half_row, axis=6), jnp.roll(even_field, -1, axis=5), jnp.roll(even_field, -1, axis=4) * ahead_sign)
    backward = (x_behind, jnp.roll(even_field, half_row, axis=6), jnp.roll(even_field, 1, axis=5), jnp.roll(even_field, 1, axis=4) * behind_sign)
    hopped = wilson_hop(forward, backward, hop_links.astype(jnp.float32))
    odd_modes = clover_apply(clover_inverse, hop_kappa * hopped).astype(jnp.bfloat16)

    def one_slice(operands):
        even_slice, odd_slice, time_value = operands
        return meson_layout(meson_block(even_slice, odd_slice, time_value, z_values, momenta))

    meson = lax.map(one_slice, (jnp.moveaxis(even_modes, 4, 0), jnp.moveaxis(odd_modes, 4, 0), t_values))
    meson = lax.optimization_barrier(meson.astype(jnp.bfloat16)).astype(jnp.float32)
    pair_weights = mode_weights[:, None] * mode_weights[None, :]
    weighted = (meson * pair_weights).reshape(NT, -1)
    flat_fields = meson.reshape(NT, -1)
    raw_pairs = jnp.dot(weighted, flat_fields.T, precision=lax.Precision.HIGHEST)
    sink_index = ((t_values[:, None] + separations) % NT).astype(jnp.int32)
    picked = jnp.take_along_axis(raw_pairs, sink_index, axis=1)
    correlator = picked * (1.0 / (16.0 * NMODE * NMOM * LS ** 3))
    return odd_modes, correlator
```

```python
import functools
import math

import jax
import jax.numpy as jnp
from jax import lax
from jax.experimental import pallas as pl
from jax.experimental.pallas import tpu as pltpu
from jax.sharding import PartitionSpec as P

NMODE = 16
NMOM = 16
LS = 16
ZL = 4
F32 = jnp.float32
BF16 = jnp.bfloat16
MESH = pl.DeviceIdType.MESH

hop_kappa = 0.125
gamma_source = ((3, 2, 1, 0), (3, 2, 1, 0), (2, 3, 0, 1), (2, 3, 0, 1))
gamma_factor = ((3, 3, 2, 2), (1, 0, 0, 1), (3, 2, 2, 3), (0, 0, 0, 0))
factor_parts = ((1, 0), (-1, 0), (0, 1), (0, -1))


def add_factor(base, value, code, sign):
    (br, bi), (vr, vi) = base, value
    re, im = factor_parts[code]
    re, im = re * sign, im * sign
    if re == 1:
        return br + vr, bi + vi
    if re == -1:
        return br - vr, bi - vi
    if im == 1:
        return br - vi, bi + vr
    return br + vi, bi - vr


def project(spin, d, sign):
    return [
        [
            add_factor(spin[s][c], spin[gamma_source[d][s]][c], gamma_factor[d][s], sign)
            for c in range(3)
        ]
        for s in range(2)
    ]


def load_spin(load):
    return [[(load(s * 3 + c), load(12 + s * 3 + c)) for c in range(3)] for s in range(4)]


def link_times(load, half, adjoint):
    out = [[None] * 3 for _ in range(2)]
    for a in range(3):
        for b in range(3):
            lr, li = (load(0, b, a), load(1, b, a)) if adjoint else (load(0, a, b), load(1, a, b))
            for s in range(2):
                hr, hi = half[s][b]
                if adjoint:
                    re, im = lr * hr + li * hi, lr * hi - li * hr
                else:
                    re, im = lr * hr - li * hi, lr * hi + li * hr
                old = out[s][a]
                out[s][a] = (re, im) if old is None else (old[0] + re, old[1] + im)
    return out


def add_hop(total, half, d, sign):
    for s in range(2):
        for c in range(3):
            total[s][c] = (total[s][c][0] + half[s][c][0], total[s][c][1] + half[s][c][1])
    for s in range(2, 4):
        for c in range(3):
            total[s][c] = add_factor(
                total[s][c], half[gamma_source[d][s]][c], gamma_factor[d][s], sign
            )
    return total


def map_half(half, f):
    return [[(f(half[s][c][0]), f(half[s][c][1])) for c in range(3)] for s in range(2)]


def halo_kernel(nt, ns, e_ref, e2_ref, ht_ref, hz_ref, ef, st, sz, ts_sem, tr_sem, zs_sem, zr_sem):
    t = lax.axis_index("ta")
    s = lax.axis_index("sa")
    t_up, t_dn = lax.rem(t + 1, nt), lax.rem(t + nt - 1, nt)
    s_up, s_dn = lax.rem(s + 1, ns), lax.rem(s + ns - 1, ns)
    partners = ((t_dn, s), (t_up, s), (t, s_dn), (t, s_up))
    barrier = pltpu.get_barrier_semaphore()
    for partner in partners:
        pl.semaphore_signal(barrier, inc=1, device_id=partner, device_id_type=MESH)

    def widen(m, carry):
        rows = pl.ds(pl.multiple_of(m * 96, 96), 96)
        ef[rows, :] = e_ref[rows, :].astype(F32)
        return carry

    lax.fori_loop(0, NMODE, widen, 0)
    sign_dn = jnp.where(t == 0, -1.0, 1.0).astype(F32)
    sign_up = jnp.where(t == nt - 1, -1.0, 1.0).astype(F32)
    copies = []
    for z in range(ZL):
        parts = []
        for g in range(2):
            parts.append(
                load_spin(
                    lambda comp: ef[pl.ds((g * 8 * 24 + comp) * 4 + z, 8, stride=96), :]
                )
            )
        both = [
            [
                tuple(
                    jnp.concatenate([parts[0][a][c][q], parts[1][a][c][q]], axis=0)
                    for q in range(2)
                )
                for c in range(3)
            ]
            for a in range(4)
        ]
        for a in range(4):
            for c in range(3):
                for q in range(2):
                    e2_ref[z, q * 12 + a * 3 + c] = both[a][c][q].astype(BF16)
        for way, sign, factor in ((0, -1, sign_dn), (1, 1, sign_up)):
            half = project(both, 3, sign)
            for a in range(2):
                for c in range(3):
                    for q in range(2):
                        st[way, z, q * 6 + a * 3 + c] = (half[a][c][q] * factor).astype(BF16)
        for edge, way, sign in ((0, 0, -1), (ZL - 1, 1, 1)):
            if z == edge:
                half = project(both, 2, sign)
                for a in range(2):
                    for c in range(3):
                        for q in range(2):
                            sz[way, q * 6 + a * 3 + c] = half[a][c][q].astype(BF16)
        if z == 0:
            pl.semaphore_wait(barrier, 4)
        for way in range(2):
            copy = pltpu.make_async_remote_copy(
                src_ref=st.at[way, z],
                dst_ref=ht_ref.at[way, z],
                send_sem=ts_sem.at[way, z],
                recv_sem=tr_sem.at[way, z],
                device_id=partners[way],
                device_id_type=MESH,
            )
            copy.start()
            copies.append(copy)
        for edge, way in ((0, 0), (ZL - 1, 1)):
            if z == edge:
                copy = pltpu.make_async_remote_copy(
                    src_ref=sz.at[way],
                    dst_ref=hz_ref.at[way],
                    send_sem=zs_sem.at[way],
                    recv_sem=zr_sem.at[way],
                    device_id=partners[2 + way],
                    device_id_type=MESH,
                )
                copy.start()
                copies.append(copy)
    for copy in copies:
        copy.wait()


def circle(step):
    fold = jnp.where(step > 8, 16 - step, step)
    low = jnp.where(fold > 4, 8 - fold, fold)
    value = jnp.where(low == 1, math.cos(math.pi / 8), 1.0).astype(F32)
    value = jnp.where(low == 2, math.cos(math.pi / 4), value).astype(F32)
    value = jnp.where(low == 3, math.cos(3 * math.pi / 8), value).astype(F32)
    value = jnp.where(low == 4, 0.0, value).astype(F32)
    return jnp.where(fold > 4, -value, value)


def phase_tables(t, s, momenta, cos_ref, sin_ref):
    lane = lax.broadcasted_iota(jnp.int32, (NMOM, 128), 1)
    y, h = lane >> 3, lane & 7
    nx, ny, nz = momenta[:, 0:1], momenta[:, 1:2], momenta[:, 2:3]
    for parity in range(2):
        for zl in range(ZL):
            z = s * ZL + zl
            x = 2 * h + ((t + z + y + parity) & 1)
            step = (nx * x + ny * y + nz * z) & 15
            cos_ref[parity, zl] = circle(step)
            sin_ref[parity, zl] = circle((step + 12) & 15)


def meson_part(modes_ref, parity, z, cos_ref, sin_ref, total_ref):
    for a in range(4):
        for c in range(3):
            comp = a * 3 + c
            vr = modes_ref[z, comp].astype(F32)
            vi = modes_ref[z, 12 + comp].astype(F32)
            rows = []
            for p in range(NMOM):
                cs = cos_ref[parity, z, pl.ds(p, 1), :]
                sn = sin_ref[parity, z, pl.ds(p, 1), :]
                rows.append(
                    jnp.concatenate(
                        [
                            (vr * cs - vi * sn).astype(BF16),
                            (-(vr * sn + vi * cs)).astype(BF16),
                        ],
                        axis=1,
                    )
                )
            left = jnp.concatenate(rows, axis=0)
            real_rows, imag_rows = [], []
            for k in range(4):
                other = gamma_source[k][a] * 3 + c
                wr = modes_ref[z, other]
                wi = modes_ref[z, 12 + other]
                re, im = factor_parts[gamma_factor[k][a]]
                if re == 1:
                    gr, gi = wr, wi
                elif re == -1:
                    gr, gi = -wr, -wi
                elif im == 1:
                    gr, gi = -wi, wr
                else:
                    gr, gi = wi, -wr
                real_rows.append(jnp.concatenate([gr, -gi], axis=1))
                imag_rows.append(jnp.concatenate([gi, gr], axis=1))
            right = jnp.concatenate(real_rows + imag_rows, axis=0)
            total_ref[...] += lax.dot_general(
                left, right, (((1,), (1,)), ((), ())), preferred_element_type=F32
            )


def field_kernel(
    e2_ref, ht_ref, hz_ref, links_ref, clover_ref, momenta_ref,
    odd_ref, total_ref,
    ef, tf, zf, lf, ob, of, cos_ref, sin_ref,
):
    t = lax.axis_index("ta")
    s = lax.axis_index("sa")
    phase_tables(t, s, momenta_ref[...], cos_ref, sin_ref)
    total_ref[...] = jnp.zeros_like(total_ref)

    def even_step(z, carry):
        meson_part(e2_ref, 0, z, cos_ref, sin_ref, total_ref)
        return carry

    lax.fori_loop(0, ZL, even_step, 0)

    def widen_links(i, carry):
        rows = pl.ds(pl.multiple_of(i * 96, 96), 96)
        lf[rows, :] = links_ref[rows, :].astype(F32)
        return carry

    lax.fori_loop(0, 6, widen_links, 0)

    def widen(z, carry):
        ef[z] = e2_ref[z].astype(F32)
        tf[0, z] = ht_ref[0, z].astype(F32)
        tf[1, z] = ht_ref[1, z].astype(F32)
        return carry

    lax.fori_loop(0, ZL, widen, 0)
    zf[0, ZL - 1] = hz_ref[0].astype(F32)
    zf[1, 0] = hz_ref[1].astype(F32)

    def z_halves(i, carry):
        z, g = i // 2, i % 2
        rows = pl.ds(pl.multiple_of(g * 8, 8), 8)
        for way, sign, source, target in ((0, -1, z + 1, z), (1, 1, z, z + 1)):
            half = project(load_spin(lambda comp: ef[source, comp, rows, :]), 2, sign)
            for a in range(2):
                for c in range(3):
                    for q in range(2):
                        zf[way, target, q * 6 + a * 3 + c, rows, :] = half[a][c][q]
        return carry

    lax.fori_loop(0, 2 * (ZL - 1), z_halves, 0)

    lane = lax.broadcasted_iota(jnp.int32, (8, 128), 1)
    first, last = (lane & 7) == 0, (lane & 7) == 7

    def hop_step(i, carry):
        z, g = i // 2, i % 2
        rows = pl.ds(pl.multiple_of(g * 8, 8), 8)
        shifted = ((t + s * ZL + z + (lane >> 3) + 1) & 1) == 1
        spin = load_spin(lambda comp: ef[z, comp, rows, :])
        zero = jnp.zeros((8, 128), F32)
        total = [[(zero, zero) for _ in range(3)] for _ in range(4)]

        def x_ahead(v):
            ahead = jnp.where(last, pltpu.roll(v, 7, 1), pltpu.roll(v, 127, 1))
            return jnp.where(shifted, ahead, v)

        def x_behind(v):
            behind = jnp.where(first, pltpu.roll(v, 121, 1), pltpu.roll(v, 1, 1))
            return jnp.where(shifted, v, behind)

        def link(way, d):
            def load(q, a, b):
                row = ((((way * 4 + d) * 2 + q) * 3 + a) * 3 + b) * ZL
                return lf[pl.ds(row + z, 1), :]

            return load

        def stored(ref, way):
            return [
                [(ref[way, z, a * 3 + c, rows, :], ref[way, z, 6 + a * 3 + c, rows, :]) for c in range(3)]
                for a in range(2)
            ]

        for way, sign in ((0, -1), (1, 1)):
            for d in range(4):
                if d == 0:
                    half = map_half(project(spin, 0, sign), (x_ahead, x_behind)[way])
                elif d == 1:
                    half = map_half(
                        project(spin, 1, sign), lambda v: pltpu.roll(v, (120, 8)[way], 1)
                    )
                else:
                    half = stored(zf if d == 2 else tf, way)
                total = add_hop(total, link_times(link(way, d), half, way == 1), d, sign)

        for chir in range(2):
            source = [
                tuple(hop_kappa * total[2 * chir + col // 3][col % 3][q] for q in range(2))
                for col in range(6)
            ]
            for r in range(6):
                out_real = out_imag = None
                for col in range(6):
                    row = ((chir * 2 * 6 + r) * 6 + col) * ZL
                    cr = clover_ref[pl.ds(row + z, 1), :]
                    ci = clover_ref[pl.ds(row + 36 * ZL + z, 1), :]
                    vr, vi = source[col]
                    re, im = cr * vr - ci * vi, cr * vi + ci * vr
                    out_real = re if out_real is None else out_real + re
                    out_imag = im if out_imag is None else out_imag + im
                place = 6 * chir + r
                for q, value in ((0, out_real), (12, out_imag)):
                    of[z, q + place, rows, :] = value
        return carry

    lax.fori_loop(0, 2 * ZL, hop_step, 0)

    def odd_step(z, carry):
        ob[z] = of[z].astype(BF16)
        meson_part(ob, 1, z, cos_ref, sin_ref, total_ref)
        return carry

    lax.fori_loop(0, ZL, odd_step, 0)
    turned = lf

    def turn(comp, carry):
        for z in range(ZL):
            for g in range(2):
                turned[pl.ds(g * 32 + z, 8, stride=4), :] = of[z, comp, pl.ds(g * 8, 8), :]
        odd_ref[:, comp] = turned[pl.ds(0, 64), :].astype(BF16).reshape(NMODE, ZL, 128)
        return carry

    lax.fori_loop(0, 24, turn, 0)


def pair_kernel(
    nt, ns, total_ref, weights_ref, sep_ref, out_ref,
    arrive, flat, rows_out, rows_in, gathered, gram, back, last,
    rs_send, rs_recv, a_send, a_recv, b_send, b_recv, l_send, l_recv,
):
    t = lax.axis_index("ta")
    s = lax.axis_index("sa")
    quarter = NMOM * NMODE // ns
    per = quarter // nt
    barrier = pltpu.get_barrier_semaphore()

    def greet(d, carry):
        pl.semaphore_signal(
            barrier, inc=1, device_id=(lax.rem(t + d, nt), s), device_id_type=MESH
        )
        return carry

    for d in range(1, ns):
        pl.semaphore_signal(
            barrier, inc=1, device_id=(t, lax.rem(s + d, ns)), device_id_type=MESH
        )
    lax.fori_loop(1, nt, greet, 0)
    pl.semaphore_wait(barrier, ns - 1 + nt - 1)

    copies = []
    for d in range(1, ns):
        partner = lax.rem(s + d, ns)
        copy = pltpu.make_async_remote_copy(
            src_ref=total_ref.at[pl.ds(pl.multiple_of(partner * quarter, quarter), quarter)],
            dst_ref=arrive.at[d - 1],
            send_sem=rs_send.at[d - 1],
            recv_sem=rs_recv.at[d - 1],
            device_id=(t, partner),
            device_id_type=MESH,
        )
        copy.start()
        copies.append(copy)
    mine = total_ref[pl.ds(pl.multiple_of(s * quarter, quarter), quarter), :]
    for d, copy in enumerate(copies):
        copy.wait()
        mine = mine + arrive[d]
    flat[pl.ds(0, quarter), :] = mine.astype(BF16).astype(F32)
    for o in range(nt):
        for r in range(per):
            rows_out[o, r] = flat[pl.ds(o * per + r, 1), :]

    def exchange(src, dst, send_sem, recv_sem):
        def send(d, carry):
            partner = lax.rem(t + d, nt)
            pltpu.make_async_remote_copy(
                src_ref=src.at[partner],
                dst_ref=dst.at[t],
                send_sem=send_sem,
                recv_sem=recv_sem,
                device_id=(partner, s),
                device_id_type=MESH,
            ).start()
            return carry

        lax.fori_loop(1, nt, send, 0)
        dst[pl.ds(t, 1)] = src[pl.ds(t, 1)]
        others = pl.ds(0, nt - 1)
        pltpu.make_async_copy(src.at[others], src.at[others], send_sem).wait()
        pltpu.make_async_copy(dst.at[others], dst.at[others], recv_sem).wait()

    exchange(rows_out, rows_in, a_send, a_recv)

    lane = lax.broadcasted_iota(jnp.int32, (NMODE, 128), 1)
    spread = (lane % NMODE == lax.broadcasted_iota(jnp.int32, (NMODE, 128), 0)).astype(F32)
    weights = weights_ref[...]
    weight_j = jnp.dot(weights, spread, precision=lax.Precision.HIGHEST, preferred_element_type=F32)
    mode = lax.broadcasted_iota(jnp.int32, (1, NMODE), 1)
    gathered[...] = jnp.zeros_like(gathered)
    product = None
    tall = max(nt, 8)
    for r in range(per):
        for k in range(nt):
            gathered[pl.ds(k, 1), :] = rows_in[k, r]
        weight_i = jnp.sum(
            jnp.where(mode == (t * per + r) % NMODE, weights, 0.0), axis=1, keepdims=True
        )
        everything = gathered[...]
        term = lax.dot_general(
            everything[:tall] * (weight_i * weight_j),
            everything,
            (((1,), (1,)), ((), ())),
            precision=lax.Precision.HIGHEST,
            preferred_element_type=F32,
        )
        product = term if product is None else product + term
    flat[pl.ds(0, tall), :] = product
    for k in range(nt):
        gram[k] = flat[pl.ds(k, 1), :]
    exchange(gram, back, b_send, b_recv)
    row = jnp.sum(back[...], axis=0)
    last[0] = row
    copies = []
    for d in range(1, ns):
        copy = pltpu.make_async_remote_copy(
            src_ref=last.at[0],
            dst_ref=last.at[d],
            send_sem=l_send.at[d - 1],
            recv_sem=l_recv.at[d - 1],
            device_id=(t, lax.rem(s + d, ns)),
            device_id_type=MESH,
        )
        copy.start()
        copies.append(copy)
    for d, copy in enumerate(copies):
        copy.wait()
        row = row + last[d + 1]
    sink = lax.rem(t + sep_ref[...], nt)
    chosen = (lax.broadcasted_iota(jnp.int32, (128, 16), 0) == sink).astype(F32)
    picked = jnp.dot(row, chosen, precision=lax.Precision.HIGHEST, preferred_element_type=F32)
    out_ref[...] = picked * (1.0 / (16.0 * NMODE * NMOM * LS**3))


def body(nt, ns, even_modes, hop_links, clover_inverse, momenta, mode_weights, separations):
    vmem = pl.BlockSpec(memory_space=pltpu.VMEM)
    limit = 48 * 1024 * 1024
    shape = jax.ShapeDtypeStruct
    dma = pltpu.SemaphoreType.DMA
    e2, ht, hz = pl.pallas_call(
        functools.partial(halo_kernel, nt, ns),
        out_shape=(
            shape((ZL, 24, NMODE, 128), BF16),
            shape((2, ZL, 12, NMODE, 128), BF16),
            shape((2, 12, NMODE, 128), BF16),
        ),
        in_specs=[vmem],
        out_specs=(vmem, vmem, vmem),
        scratch_shapes=[
            pltpu.VMEM((NMODE * 24 * ZL, 128), F32),
            pltpu.VMEM((2, ZL, 12, NMODE, 128), BF16),
            pltpu.VMEM((2, 12, NMODE, 128), BF16),
            dma((2, ZL)), dma((2, ZL)), dma((2,)), dma((2,)),
        ],
        compiler_params=pltpu.CompilerParams(
            collective_id=0, has_side_effects=True, vmem_limit_bytes=limit
        ),
        name="halo",
    )(even_modes.reshape(NMODE * 24 * ZL, 128))
    odd_modes, total = pl.pallas_call(
        field_kernel,
        out_shape=(
            shape((NMODE, 24, ZL, 128), BF16),
            shape((NMOM * NMODE, 128), F32),
        ),
        in_specs=[vmem] * 6,
        out_specs=(vmem, vmem),
        scratch_shapes=[
            pltpu.VMEM((ZL, 24, NMODE, 128), F32),
            pltpu.VMEM((2, ZL, 12, NMODE, 128), F32),
            pltpu.VMEM((2, ZL, 12, NMODE, 128), F32),
            pltpu.VMEM((144 * ZL, 128), F32),
            pltpu.VMEM((ZL, 24, NMODE, 128), BF16),
            pltpu.VMEM((ZL, 24, NMODE, 128), F32),
            pltpu.VMEM((2, ZL, NMOM, 128), F32),
            pltpu.VMEM((2, ZL, NMOM, 128), F32),
        ],
        compiler_params=pltpu.CompilerParams(vmem_limit_bytes=limit),
        name="fields",
    )(e2, ht, hz, hop_links.reshape(144 * ZL, 128), clover_inverse.reshape(144 * ZL, 128), momenta)
    quarter = NMOM * NMODE // ns
    per = quarter // nt
    correlator = pl.pallas_call(
        functools.partial(pair_kernel, nt, ns),
        out_shape=shape((1, 16), F32),
        in_specs=[vmem] * 3,
        out_specs=vmem,
        scratch_shapes=[
            pltpu.VMEM((ns - 1, quarter, 128), F32),
            pltpu.VMEM((max(quarter, nt), 128), F32),
            pltpu.VMEM((nt, per, 1, 128), F32),
            pltpu.VMEM((nt, per, 1, 128), F32),
            pltpu.VMEM((128, 128), F32),
            pltpu.VMEM((nt, 1, 128), F32),
            pltpu.VMEM((nt, 1, 128), F32),
            pltpu.VMEM((ns, 1, 128), F32),
            dma((ns - 1,)), dma((ns - 1,)), dma, dma, dma, dma, dma((ns - 1,)), dma((ns - 1,)),
        ],
        compiler_params=pltpu.CompilerParams(
            collective_id=1, has_side_effects=True, vmem_limit_bytes=limit
        ),
        name="pairs",
    )(total, mode_weights.reshape(1, NMODE), separations)
    return odd_modes.reshape(even_modes.shape), correlator


def solution(mesh):
    in_specs = (
        P(None, None, None, None, "ta", "sa", None),
        P(None, None, None, None, None, "ta", "sa", None),
        P(None, None, None, None, "ta", "sa", None),
        P(),
        P(),
        P("ta", None),
    )
    out_specs = (P(None, None, None, None, "ta", "sa", None), P("ta", None))
    return jax.shard_map(
        functools.partial(body, mesh.shape["ta"], mesh.shape["sa"]),
        mesh=mesh,
        in_specs=in_specs,
        out_specs=out_specs,
        check_vma=False,
    )
```

```python
import functools
import math

import jax
import jax.numpy as jnp
from jax import lax
from jax.experimental import pallas as pl
from jax.experimental.pallas import tpu as pltpu
from jax.sharding import PartitionSpec as P

NMODE = 16
NMOM = 16
LS = 16
ZL = 4
F32 = jnp.float32
BF16 = jnp.bfloat16
MESH = pl.DeviceIdType.MESH

hop_kappa = 0.125
gamma_source = ((3, 2, 1, 0), (3, 2, 1, 0), (2, 3, 0, 1), (2, 3, 0, 1))
gamma_factor = ((3, 3, 2, 2), (1, 0, 0, 1), (3, 2, 2, 3), (0, 0, 0, 0))
factor_parts = ((1, 0), (-1, 0), (0, 1), (0, -1))


def add_factor(base, value, code, sign):
    (br, bi), (vr, vi) = base, value
    re, im = factor_parts[code]
    re, im = re * sign, im * sign
    if re == 1:
        return br + vr, bi + vi
    if re == -1:
        return br - vr, bi - vi
    if im == 1:
        return br - vi, bi + vr
    return br + vi, bi - vr


def project(spin, d, sign):
    return [
        [
            add_factor(spin[s][c], spin[gamma_source[d][s]][c], gamma_factor[d][s], sign)
            for c in range(3)
        ]
        for s in range(2)
    ]


def load_spin(load):
    return [[(load(s * 3 + c), load(12 + s * 3 + c)) for c in range(3)] for s in range(4)]


def link_times(load, half, adjoint):
    out = [[None] * 3 for _ in range(2)]
    for a in range(3):
        for b in range(3):
            lr, li = (load(0, b, a), load(1, b, a)) if adjoint else (load(0, a, b), load(1, a, b))
            for s in range(2):
                hr, hi = half[s][b]
                if adjoint:
                    re, im = lr * hr + li * hi, lr * hi - li * hr
                else:
                    re, im = lr * hr - li * hi, lr * hi + li * hr
                old = out[s][a]
                out[s][a] = (re, im) if old is None else (old[0] + re, old[1] + im)
    return out


def add_hop(total, half, d, sign):
    for s in range(2):
        for c in range(3):
            total[s][c] = (total[s][c][0] + half[s][c][0], total[s][c][1] + half[s][c][1])
    for s in range(2, 4):
        for c in range(3):
            total[s][c] = add_factor(
                total[s][c], half[gamma_source[d][s]][c], gamma_factor[d][s], sign
            )
    return total


def map_half(half, f):
    return [[(f(half[s][c][0]), f(half[s][c][1])) for c in range(3)] for s in range(2)]


def circle(step):
    fold = jnp.where(step > 8, 16 - step, step)
    low = jnp.where(fold > 4, 8 - fold, fold)
    value = jnp.where(low == 1, math.cos(math.pi / 8), 1.0).astype(F32)
    value = jnp.where(low == 2, math.cos(math.pi / 4), value).astype(F32)
    value = jnp.where(low == 3, math.cos(3 * math.pi / 8), value).astype(F32)
    value = jnp.where(low == 4, 0.0, value).astype(F32)
    return jnp.where(fold > 4, -value, value)


def phase_tables(t, s, momenta, cos_ref, sin_ref):
    lane = lax.broadcasted_iota(jnp.int32, (NMOM, 128), 1)
    y, h = lane >> 3, lane & 7
    place = lax.broadcasted_iota(jnp.int32, (NMOM, NMOM), 1)
    diagonal = place == lax.broadcasted_iota(jnp.int32, (NMOM, NMOM), 0)
    nx, ny, nz = (
        jnp.sum(
            jnp.where(diagonal, momenta[d : d + 1, :].astype(F32), 0.0), axis=1, keepdims=True
        ).astype(jnp.int32)
        for d in range(3)
    )
    for parity in range(2):
        for zl in range(ZL):
            z = s * ZL + zl
            x = 2 * h + ((t + z + y + parity) & 1)
            step = (nx * x + ny * y + nz * z) & 15
            cos_ref[parity, zl] = circle(step)
            sin_ref[parity, zl] = circle((step + 12) & 15)


def meson_part(modes_ref, parity, z, cos_ref, sin_ref, total_ref):
    for a in range(4):
        for c in range(3):
            comp = a * 3 + c
            vr = modes_ref[z, comp].astype(F32)
            vi = modes_ref[z, 12 + comp].astype(F32)
            rows = []
            for p in range(NMOM):
                cs = cos_ref[parity, z, pl.ds(p, 1), :]
                sn = sin_ref[parity, z, pl.ds(p, 1), :]
                rows.append(
                    jnp.concatenate(
                        [
                            (vr * cs - vi * sn).astype(BF16),
                            (-(vr * sn + vi * cs)).astype(BF16),
                        ],
                        axis=1,
                    )
                )
            left = jnp.concatenate(rows, axis=0)
            real_rows, imag_rows = [], []
            for k in range(4):
                other = gamma_source[k][a] * 3 + c
                wr = modes_ref[z, other]
                wi = modes_ref[z, 12 + other]
                re, im = factor_parts[gamma_factor[k][a]]
                if re == 1:
                    gr, gi = wr, wi
                elif re == -1:
                    gr, gi = -wr, -wi
                elif im == 1:
                    gr, gi = -wi, wr
                else:
                    gr, gi = wi, -wr
                real_rows.append(jnp.concatenate([gr, -gi], axis=1))
                imag_rows.append(jnp.concatenate([gi, gr], axis=1))
            right = jnp.concatenate(real_rows + imag_rows, axis=0)
            total_ref[...] += lax.dot_general(
                left, right, (((1,), (1,)), ((), ())), preferred_element_type=F32
            )


def kernel(
    nt, ns,
    e_hbm, links_hbm, clover_hbm, momenta_hbm, weights_hbm, sep_hbm,
    odd_ref, out_ref,
    e_ref, links_ref, clover_ref, momenta_ref, weights_ref, sep_ref,
    ef, ewide, e2, st, sz, ht, hz, tf, zf, lf, of, ob, cos_ref, sin_ref,
    total_ref, arr1, turn2, send2, arr2, gathered, send3, arr3, send4, arr4,
    in_sem, ts_sem, tr_sem, zs_sem, zr_sem, x_send, x_recv,
):
    t = lax.axis_index("ta")
    s = lax.axis_index("sa")
    tz, ty, tx = t // 8, lax.rem(t, 8) // 2, lax.rem(t, 2)
    t_up, t_dn = lax.rem(t + 1, nt), lax.rem(t + nt - 1, nt)
    s_up, s_dn = lax.rem(s + 1, ns), lax.rem(s + ns - 1, ns)
    partners = ((t_dn, s), (t_up, s), (t, s_dn), (t, s_up))
    mine_a = ty * 4 + s
    mine_b = tz * 2 + tx

    def member_a(index):
        return tz * 8 + (index // 4) * 2 + tx, lax.rem(index, 4)

    def member_b(index):
        return (index // 2) * 8 + ty * 2 + lax.rem(index, 2), s

    groups = ((mine_a, member_a), (mine_b, member_b))
    loads = []
    for i, (source, target) in enumerate(
        (
            (e_hbm, e_ref), (momenta_hbm, momenta_ref), (links_hbm, links_ref),
            (clover_hbm, clover_ref), (weights_hbm, weights_ref), (sep_hbm, sep_ref),
        )
    ):
        load = pltpu.make_async_copy(source, target, in_sem.at[i])
        load.start()
        loads.append(load)
    barrier = pltpu.get_barrier_semaphore()
    for partner in partners[:2]:
        pl.semaphore_signal(barrier, inc=1, device_id=partner, device_id_type=MESH)
    for mine, member in groups:
        def greet(d, carry, mine=mine, member=member):
            pl.semaphore_signal(
                barrier, inc=1, device_id=member(lax.rem(mine + d, 16)), device_id_type=MESH
            )
            return carry

        lax.fori_loop(1, 16, greet, 0)

    loads[0].wait()

    def widen(m, carry):
        rows = pl.ds(pl.multiple_of(m * 96, 96), 96)
        ewide[rows, :] = e_ref[rows, :].astype(F32)
        return carry

    lax.fori_loop(0, NMODE, widen, 0)
    sign_dn = jnp.where(t == 0, -1.0, 1.0).astype(F32)
    sign_up = jnp.where(t == nt - 1, -1.0, 1.0).astype(F32)

    def t_copy(way, z):
        return pltpu.make_async_remote_copy(
            src_ref=st.at[way, z],
            dst_ref=ht.at[way, z],
            send_sem=ts_sem.at[way, z],
            recv_sem=tr_sem.at[way, z],
            device_id=partners[way],
            device_id_type=MESH,
        )

    def z_copy(way):
        return pltpu.make_async_remote_copy(
            src_ref=sz.at[way],
            dst_ref=hz.at[way],
            send_sem=zs_sem.at[way],
            recv_sem=zr_sem.at[way],
            device_id=partners[2 + way],
            device_id_type=MESH,
        )

    def prepare(z):
        halves = []
        for g in range(2):
            halves.append(
                load_spin(
                    lambda comp: ewide[pl.ds((g * 8 * 24 + comp) * 4 + z, 8, stride=96), :]
                )
            )
        both = [
            [
                tuple(
                    jnp.concatenate([halves[0][a][c][q], halves[1][a][c][q]], axis=0)
                    for q in range(2)
                )
                for c in range(3)
            ]
            for a in range(4)
        ]
        for way, sign, factor in ((0, -1, sign_dn), (1, 1, sign_up)):
            half = project(both, 3, sign)
            for a in range(2):
                for c in range(3):
                    for q in range(2):
                        st[way, z, q * 6 + a * 3 + c] = (half[a][c][q] * factor).astype(BF16)
        for edge, way, sign in ((0, 0, -1), (ZL - 1, 1, 1)):
            if z == edge:
                half = project(both, 2, sign)
                for a in range(2):
                    for c in range(3):
                        for q in range(2):
                            sz[way, q * 6 + a * 3 + c] = half[a][c][q].astype(BF16)
        for a in range(4):
            for c in range(3):
                for q in range(2):
                    ef[z, q * 12 + a * 3 + c] = both[a][c][q]
                    e2[z, q * 12 + a * 3 + c] = both[a][c][q].astype(BF16)

    for z in range(ZL):
        prepare(z)
        if z == 0:
            pl.semaphore_wait(barrier, 32)
            z_copy(0).start()
        for way in range(2):
            t_copy(way, z).start()
    z_copy(1).start()

    loads[1].wait()
    phase_tables(t, s, momenta_ref[...], cos_ref, sin_ref)
    total_ref[...] = jnp.zeros_like(total_ref)

    def even_step(z, carry):
        meson_part(e2, 0, z, cos_ref, sin_ref, total_ref)
        return carry

    lax.fori_loop(0, ZL, even_step, 0)
    loads[2].wait()

    def widen_links(i, carry):
        rows = pl.ds(pl.multiple_of(i * 96, 96), 96)
        lf[rows, :] = links_ref[rows, :].astype(F32)
        return carry

    lax.fori_loop(0, 6, widen_links, 0)

    def z_halves(i, carry):
        z, g = i // 2, lax.rem(i, 2)
        rows = pl.ds(pl.multiple_of(g * 8, 8), 8)
        for way, sign, source, target in ((0, -1, z + 1, z), (1, 1, z, z + 1)):
            half = project(load_spin(lambda comp: ef[source, comp, rows, :]), 2, sign)
            for a in range(2):
                for c in range(3):
                    for q in range(2):
                        zf[way, target, q * 6 + a * 3 + c, rows, :] = half[a][c][q]
        return carry

    lax.fori_loop(0, 2 * (ZL - 1), z_halves, 0)
    for way in range(2):
        z_copy(way).wait_recv()
    zf[0, ZL - 1] = hz[0].astype(F32)
    zf[1, 0] = hz[1].astype(F32)
    lane = lax.broadcasted_iota(jnp.int32, (8, 128), 1)
    first, last = (lane & 7) == 0, (lane & 7) == 7

    def link(way, d, z):
        def load(q, a, b):
            row = ((((way * 4 + d) * 2 + q) * 3 + a) * 3 + b) * ZL
            return lf[pl.ds(row + z, 1), :]

        return load

    def stored(read):
        return [[(read(a * 3 + c), read(6 + a * 3 + c)) for c in range(3)] for a in range(2)]

    def near_step(i, carry):
        z, g = i // 2, lax.rem(i, 2)
        rows = pl.ds(pl.multiple_of(g * 8, 8), 8)
        shifted = ((t + s * ZL + z + (lane >> 3) + 1) & 1) == 1
        spin = load_spin(lambda comp: ef[z, comp, rows, :])
        zero = jnp.zeros((8, 128), F32)
        total = [[(zero, zero) for _ in range(3)] for _ in range(4)]

        def x_ahead(v):
            ahead = jnp.where(last, pltpu.roll(v, 7, 1), pltpu.roll(v, 127, 1))
            return jnp.where(shifted, ahead, v)

        def x_behind(v):
            behind = jnp.where(first, pltpu.roll(v, 121, 1), pltpu.roll(v, 1, 1))
            return jnp.where(shifted, v, behind)

        for way, sign in ((0, -1), (1, 1)):
            for d in range(3):
                if d == 0:
                    half = map_half(project(spin, 0, sign), (x_ahead, x_behind)[way])
                elif d == 1:
                    half = map_half(
                        project(spin, 1, sign), lambda v: pltpu.roll(v, (120, 8)[way], 1)
                    )
                else:
                    half = stored(lambda comp: zf[way, z, comp, rows, :])
                total = add_hop(total, link_times(link(way, d, z), half, way == 1), d, sign)
        for a in range(4):
            for c in range(3):
                for q in range(2):
                    of[z, q * 12 + a * 3 + c, rows, :] = total[a][c][q]
        return carry

    lax.fori_loop(0, 2 * ZL, near_step, 0)
    loads[3].wait()

    def far_step(z, carry):
        for way in range(2):
            t_copy(way, z).wait_recv()
            tf[way] = ht[way, z].astype(F32)

        def group_step(g, carry):
            rows = pl.ds(pl.multiple_of(g * 8, 8), 8)
            total = load_spin(lambda comp: of[z, comp, rows, :])
            for way, sign in ((0, -1), (1, 1)):
                half = stored(lambda comp: tf[way, comp, rows, :])
                total = add_hop(total, link_times(link(way, 3, z), half, way == 1), 3, sign)
            for chir in range(2):
                source = [
                    tuple(hop_kappa * total[2 * chir + col // 3][col % 3][q] for q in range(2))
                    for col in range(6)
                ]
                for r in range(6):
                    out_real = out_imag = None
                    for col in range(6):
                        row = ((chir * 2 * 6 + r) * 6 + col) * ZL
                        cr = clover_ref[pl.ds(row + z, 1), :]
                        ci = clover_ref[pl.ds(row + 36 * ZL + z, 1), :]
                        vr, vi = source[col]
                        re, im = cr * vr - ci * vi, cr * vi + ci * vr
                        out_real = re if out_real is None else out_real + re
                        out_imag = im if out_imag is None else out_imag + im
                    place = 6 * chir + r
                    of[z, place, rows, :] = out_real
                    of[z, 12 + place, rows, :] = out_imag
            return carry

        lax.fori_loop(0, 2, group_step, 0)
        ob[z] = of[z].astype(BF16)
        meson_part(ob, 1, z, cos_ref, sin_ref, total_ref)
        return carry

    lax.fori_loop(0, ZL, far_step, 0)

    def send(stage, group, source, target):
        mine, member = group

        def one(d, carry):
            other = lax.rem(mine + d, 16)
            pltpu.make_async_remote_copy(
                src_ref=source(other),
                dst_ref=target.at[mine],
                send_sem=x_send.at[stage],
                recv_sem=x_recv.at[stage],
                device_id=member(other),
                device_id_type=MESH,
            ).start()
            return carry

        lax.fori_loop(1, 16, one, 0)

    def wait(stage, target, sems):
        others = target.at[pl.ds(0, 15)]
        pltpu.make_async_copy(others, others, sems.at[stage]).wait()

    def rows_a(index):
        return pl.ds(pl.multiple_of(index * 16, 16), 16)

    send(0, groups[0], lambda i: total_ref.at[rows_a(i)], arr1)
    arr1[mine_a] = total_ref[rows_a(mine_a), :]

    def turn(comp, carry):
        for z in range(ZL):
            for g in range(2):
                lf[pl.ds(g * 32 + z, 8, stride=4), :] = of[z, comp, pl.ds(g * 8, 8), :]
        odd_ref[:, comp] = lf[pl.ds(0, 64), :].astype(BF16).reshape(NMODE, ZL, 128)
        return carry

    lax.fori_loop(0, 24, turn, 0)
    loads[4].wait()
    loads[5].wait()
    wait(0, arr1, x_recv)
    for y in range(4):
        field = arr1[4 * y] + arr1[4 * y + 1] + arr1[4 * y + 2] + arr1[4 * y + 3]
        field = field.astype(BF16).astype(F32)
        for g in range(2):
            turn2[pl.ds(g * 32 + y, 8, stride=4), :] = field[g * 8 : g * 8 + 8]
    for i in range(16):
        send2[i] = turn2[pl.ds(i * 4, 4), :]
    send(1, groups[1], lambda i: send2.at[i], arr2)
    arr2[mine_b] = send2[mine_b]
    weights = weights_ref[...]
    lane16 = lax.broadcasted_iota(jnp.int32, (NMODE, 128), 1)
    spread = (lane16 % NMODE == lax.broadcasted_iota(jnp.int32, (NMODE, 128), 0)).astype(F32)
    weight_j = jnp.dot(weights, spread, precision=lax.Precision.HIGHEST, preferred_element_type=F32)
    mode = lax.broadcasted_iota(jnp.int32, (1, NMODE), 1)
    weight_i = jnp.sum(jnp.where(mode == mine_b, weights, 0.0), axis=1, keepdims=True)
    pair_weight = weight_i * weight_j
    gathered[...] = jnp.zeros_like(gathered)
    wait(1, arr2, x_recv)
    for i in range(16):
        gathered[pl.ds(i * 4, 4), :] = arr2[i]
    everything = gathered[...]
    product = lax.dot_general(
        everything[:64] * pair_weight,
        everything,
        (((1,), (1,)), ((), ())),
        precision=lax.Precision.HIGHEST,
        preferred_element_type=F32,
    )
    turn2[...] = product
    for i in range(16):
        send3[i] = turn2[pl.ds(i * 4, 4), :]
    send(2, groups[1], lambda i: send3.at[i], arr3)
    arr3[mine_b] = send3[mine_b]
    wait(2, arr3, x_recv)
    part = jnp.sum(arr3[...], axis=0)
    for y in range(4):
        send4[y] = part[y : y + 1]
    send(3, groups[0], lambda i: send4.at[i // 4], arr4)
    arr4[mine_a] = send4[ty]
    sink = lax.rem(t + sep_ref[...], nt)
    column = (sink // 8 * 2 + lax.rem(sink, 2)) * 4 + lax.rem(sink, 8) // 2
    chosen = (lax.broadcasted_iota(jnp.int32, (128, 16), 0) == column).astype(F32)
    wait(3, arr4, x_recv)
    row = jnp.sum(arr4[...], axis=0)
    picked = jnp.dot(row, chosen, precision=lax.Precision.HIGHEST, preferred_element_type=F32)
    out_ref[...] = picked * (1.0 / (16.0 * NMODE * NMOM * LS**3))
    for way in range(2):
        z_copy(way).wait_send()
        for z in range(ZL):
            t_copy(way, z).wait_send()
    for stage, target in enumerate((arr1, arr2, arr3, arr4)):
        wait(stage, target, x_send)


def body(nt, ns, even_modes, hop_links, clover_inverse, momenta, mode_weights, separations):
    vmem = pl.BlockSpec(memory_space=pltpu.VMEM)
    hbm = pl.BlockSpec(memory_space=pltpu.HBM)
    shape = jax.ShapeDtypeStruct
    dma = pltpu.SemaphoreType.DMA
    sites = (ZL, 24, NMODE, 128)
    odd_modes, correlator = pl.pallas_call(
        functools.partial(kernel, nt, ns),
        out_shape=(shape((NMODE, 24, ZL, 128), BF16), shape((1, 16), F32)),
        in_specs=[hbm] * 6,
        out_specs=(vmem, vmem),
        scratch_shapes=[
            pltpu.VMEM((NMODE * 24 * ZL, 128), BF16),
            pltpu.VMEM((144 * ZL, 128), BF16),
            pltpu.VMEM((144 * ZL, 128), F32),
            pltpu.VMEM((3, NMOM), jnp.int32),
            pltpu.VMEM((1, NMODE), F32),
            pltpu.VMEM((1, 16), jnp.int32),
            pltpu.VMEM(sites, F32),
            pltpu.VMEM((NMODE * 24 * ZL, 128), F32),
            pltpu.VMEM(sites, BF16),
            pltpu.VMEM((2, ZL, 12, NMODE, 128), BF16),
            pltpu.VMEM((2, 12, NMODE, 128), BF16),
            pltpu.VMEM((2, ZL, 12, NMODE, 128), BF16),
            pltpu.VMEM((2, 12, NMODE, 128), BF16),
            pltpu.VMEM((2, 12, NMODE, 128), F32),
            pltpu.VMEM((2, ZL, 12, NMODE, 128), F32),
            pltpu.VMEM((144 * ZL, 128), F32),
            pltpu.VMEM(sites, F32),
            pltpu.VMEM(sites, BF16),
            pltpu.VMEM((2, ZL, NMOM, 128), F32),
            pltpu.VMEM((2, ZL, NMOM, 128), F32),
            pltpu.VMEM((NMOM * NMODE, 128), F32),
            pltpu.VMEM((16, 16, 128), F32),
            pltpu.VMEM((64, 128), F32),
            pltpu.VMEM((16, 4, 128), F32),
            pltpu.VMEM((16, 4, 128), F32),
            pltpu.VMEM((128, 128), F32),
            pltpu.VMEM((16, 4, 128), F32),
            pltpu.VMEM((16, 4, 128), F32),
            pltpu.VMEM((4, 1, 128), F32),
            pltpu.VMEM((16, 1, 128), F32),
            dma((6,)), dma((2, ZL)), dma((2, ZL)), dma((2,)), dma((2,)), dma((4,)), dma((4,)),
        ],
        compiler_params=pltpu.CompilerParams(
            collective_id=0, has_side_effects=True, vmem_limit_bytes=63 * 1024 * 1024
        ),
        name="correlator",
    )(
        even_modes.reshape(NMODE * 24 * ZL, 128),
        hop_links.reshape(144 * ZL, 128),
        clover_inverse.reshape(144 * ZL, 128),
        momenta.T,
        mode_weights.reshape(1, NMODE),
        separations,
    )
    return odd_modes.reshape(even_modes.shape), correlator


def solution(mesh):
    in_specs = (
        P(None, None, None, None, "ta", "sa", None),
        P(None, None, None, None, None, "ta", "sa", None),
        P(None, None, None, None, "ta", "sa", None),
        P(),
        P(),
        P("ta", None),
    )
    out_specs = (P(None, None, None, None, "ta", "sa", None), P("ta", None))
    return jax.shard_map(
        functools.partial(body, mesh.shape["ta"], mesh.shape["sa"]),
        mesh=mesh,
        in_specs=in_specs,
        out_specs=out_specs,
        check_vma=False,
    )
```

```python
import functools
import math

import jax
import jax.numpy as jnp
from jax import lax
from jax.experimental import pallas as pl
from jax.experimental.pallas import tpu as pltpu
from jax.sharding import PartitionSpec as P

NMODE = 16
NMOM = 16
LS = 16
ZL = 4
F32 = jnp.float32
BF16 = jnp.bfloat16
MESH = pl.DeviceIdType.MESH

hop_kappa = 0.125
gamma_source = ((3, 2, 1, 0), (3, 2, 1, 0), (2, 3, 0, 1), (2, 3, 0, 1))
gamma_factor = ((3, 3, 2, 2), (1, 0, 0, 1), (3, 2, 2, 3), (0, 0, 0, 0))
factor_parts = ((1, 0), (-1, 0), (0, 1), (0, -1))


def add_factor(base, value, code, sign):
    (br, bi), (vr, vi) = base, value
    re, im = factor_parts[code]
    re, im = re * sign, im * sign
    if re == 1:
        return br + vr, bi + vi
    if re == -1:
        return br - vr, bi - vi
    if im == 1:
        return br - vi, bi + vr
    return br + vi, bi - vr


def project(spin, d, sign):
    return [
        [
            add_factor(spin[s][c], spin[gamma_source[d][s]][c], gamma_factor[d][s], sign)
            for c in range(3)
        ]
        for s in range(2)
    ]


def load_spin(load):
    return [[(load(s * 3 + c), load(12 + s * 3 + c)) for c in range(3)] for s in range(4)]


def link_times(load, half, adjoint):
    out = [[None] * 3 for _ in range(2)]
    for a in range(3):
        for b in range(3):
            lr, li = (load(0, b, a), load(1, b, a)) if adjoint else (load(0, a, b), load(1, a, b))
            for s in range(2):
                hr, hi = half[s][b]
                if adjoint:
                    re, im = lr * hr + li * hi, lr * hi - li * hr
                else:
                    re, im = lr * hr - li * hi, lr * hi + li * hr
                old = out[s][a]
                out[s][a] = (re, im) if old is None else (old[0] + re, old[1] + im)
    return out


def add_hop(total, half, d, sign):
    for s in range(2):
        for c in range(3):
            total[s][c] = (total[s][c][0] + half[s][c][0], total[s][c][1] + half[s][c][1])
    for s in range(2, 4):
        for c in range(3):
            total[s][c] = add_factor(
                total[s][c], half[gamma_source[d][s]][c], gamma_factor[d][s], sign
            )
    return total


def map_half(half, f):
    return [[(f(half[s][c][0]), f(half[s][c][1])) for c in range(3)] for s in range(2)]


def circle(step):
    fold = jnp.where(step > 8, 16 - step, step)
    low = jnp.where(fold > 4, 8 - fold, fold)
    value = jnp.where(low == 1, math.cos(math.pi / 8), 1.0).astype(F32)
    value = jnp.where(low == 2, math.cos(math.pi / 4), value).astype(F32)
    value = jnp.where(low == 3, math.cos(3 * math.pi / 8), value).astype(F32)
    value = jnp.where(low == 4, 0.0, value).astype(F32)
    return jnp.where(fold > 4, -value, value)


def phase_tables(t, s, momenta, cos_ref, sin_ref):
    lane = lax.broadcasted_iota(jnp.int32, (NMOM, 128), 1)
    y, h = lane >> 3, lane & 7
    place = lax.broadcasted_iota(jnp.int32, (NMOM, NMOM), 1)
    diagonal = place == lax.broadcasted_iota(jnp.int32, (NMOM, NMOM), 0)
    nx, ny, nz = (
        jnp.sum(
            jnp.where(diagonal, momenta[d : d + 1, :].astype(F32), 0.0), axis=1, keepdims=True
        ).astype(jnp.int32)
        for d in range(3)
    )
    for parity in range(2):
        for zl in range(ZL):
            z = s * ZL + zl
            x = 2 * h + ((t + z + y + parity) & 1)
            step = (nx * x + ny * y + nz * z) & 15
            cos_ref[parity, zl] = circle(step)
            sin_ref[parity, zl] = circle((step + 12) & 15)


def meson_part(modes_ref, parity, z, cos_ref, sin_ref, total_ref):
    for a in range(4):
        for c in range(3):
            comp = a * 3 + c
            vr = modes_ref[z, comp].astype(F32)
            vi = modes_ref[z, 12 + comp].astype(F32)
            rows = []
            for p in range(NMOM):
                cs = cos_ref[parity, z, pl.ds(p, 1), :]
                sn = sin_ref[parity, z, pl.ds(p, 1), :]
                rows.append(
                    jnp.concatenate(
                        [
                            (vr * cs - vi * sn).astype(BF16),
                            (-(vr * sn + vi * cs)).astype(BF16),
                        ],
                        axis=1,
                    )
                )
            left = jnp.concatenate(rows, axis=0)
            real_rows, imag_rows = [], []
            for k in range(4):
                other = gamma_source[k][a] * 3 + c
                wr = modes_ref[z, other]
                wi = modes_ref[z, 12 + other]
                re, im = factor_parts[gamma_factor[k][a]]
                if re == 1:
                    gr, gi = wr, wi
                elif re == -1:
                    gr, gi = -wr, -wi
                elif im == 1:
                    gr, gi = -wi, wr
                else:
                    gr, gi = wi, -wr
                real_rows.append(jnp.concatenate([gr, -gi], axis=1))
                imag_rows.append(jnp.concatenate([gi, gr], axis=1))
            right = jnp.concatenate(real_rows + imag_rows, axis=0)
            total_ref[...] += lax.dot_general(
                left, right, (((1,), (1,)), ((), ())), preferred_element_type=F32
            )


def plane_distance(step):
    dy, dx, dn, dc = step
    return -(min(dy, 4 - dy) + (2 * dx if not dn else 1)), -dc


plane_steps = sorted(
    [
        (dy, dx, dn, dc)
        for dy in range(4)
        for dx in range(2)
        for dn in range(2)
        for dc in range(2)
        if dy or dx or dn or dc
    ],
    key=plane_distance,
)
ring_steps = (4, 3, 5, 2, 6, 1, 7)


def kernel(
    nt, ns,
    e_hbm, links_hbm, clover_hbm, momenta_hbm, weights_hbm, sep_hbm,
    odd_ref, out_ref,
    e_ref, links_ref, clover_ref, momenta_ref, weights_ref, sep_ref,
    ef, ewide, e2, st, sz, ht, hz, tf, zf, lf, of, ob, cos_ref, sin_ref,
    total_ref, arr1, turn2, send2, arr2, gathered, send3, arr3,
    in_sem, ts_sem, tr_sem, zs_sem, zr_sem, x_send, x_recv,
):
    t = lax.axis_index("ta")
    s = lax.axis_index("sa")
    tz, ty, tx = t // 8, lax.rem(t, 8) // 2, lax.rem(t, 2)
    t_up, t_dn = lax.rem(t + 1, nt), lax.rem(t + nt - 1, nt)
    s_up, s_dn = lax.rem(s + 1, ns), lax.rem(s + ns - 1, ns)
    partners = ((t_dn, s), (t_up, s), (t, s_dn), (t, s_up))
    place = lax.rem(t, 8) * 4 + s

    def in_plane(step):
        dy, dx, dn, dc = step
        x_half, x_near, core = lax.rem(tx + dx, 2), lax.rem(s // 2 + dn, 2), lax.rem(s + dc, 2)
        return tz * 8 + lax.rem(ty + dy, 4) * 2 + x_half, x_near * 2 + core

    def along_planes(step):
        return lax.rem(tz + step, 8) * 8 + lax.rem(t, 8), s

    loads = []
    for i, (source, target) in enumerate(
        (
            (e_hbm, e_ref), (momenta_hbm, momenta_ref), (links_hbm, links_ref),
            (clover_hbm, clover_ref), (weights_hbm, weights_ref), (sep_hbm, sep_ref),
        )
    ):
        load = pltpu.make_async_copy(source, target, in_sem.at[i])
        load.start()
        loads.append(load)
    barrier = pltpu.get_barrier_semaphore()
    for partner in partners[:2]:
        pl.semaphore_signal(barrier, inc=1, device_id=partner, device_id_type=MESH)
    for step in plane_steps:
        pl.semaphore_signal(barrier, inc=1, device_id=in_plane(step), device_id_type=MESH)
    for step in ring_steps:
        pl.semaphore_signal(barrier, inc=1, device_id=along_planes(step), device_id_type=MESH)

    loads[0].wait()

    def widen(m, carry):
        rows = pl.ds(pl.multiple_of(m * 96, 96), 96)
        ewide[rows, :] = e_ref[rows, :].astype(F32)
        return carry

    lax.fori_loop(0, NMODE, widen, 0)
    sign_dn = jnp.where(t == 0, -1.0, 1.0).astype(F32)
    sign_up = jnp.where(t == nt - 1, -1.0, 1.0).astype(F32)

    def t_copy(way, z):
        return pltpu.make_async_remote_copy(
            src_ref=st.at[way, z],
            dst_ref=ht.at[way, z],
            send_sem=ts_sem.at[way, z],
            recv_sem=tr_sem.at[way, z],
            device_id=partners[way],
            device_id_type=MESH,
        )

    def z_copy(way):
        return pltpu.make_async_remote_copy(
            src_ref=sz.at[way],
            dst_ref=hz.at[way],
            send_sem=zs_sem.at[way],
            recv_sem=zr_sem.at[way],
            device_id=partners[2 + way],
            device_id_type=MESH,
        )

    def prepare(z):
        halves = []
        for g in range(2):
            halves.append(
                load_spin(
                    lambda comp: ewide[pl.ds((g * 8 * 24 + comp) * 4 + z, 8, stride=96), :]
                )
            )
        both = [
            [
                tuple(
                    jnp.concatenate([halves[0][a][c][q], halves[1][a][c][q]], axis=0)
                    for q in range(2)
                )
                for c in range(3)
            ]
            for a in range(4)
        ]
        for way, sign, factor in ((0, -1, sign_dn), (1, 1, sign_up)):
            half = project(both, 3, sign)
            for a in range(2):
                for c in range(3):
                    for q in range(2):
                        st[way, z, q * 6 + a * 3 + c] = (half[a][c][q] * factor).astype(BF16)
        for edge, way, sign in ((0, 0, -1), (ZL - 1, 1, 1)):
            if z == edge:
                half = project(both, 2, sign)
                for a in range(2):
                    for c in range(3):
                        for q in range(2):
                            sz[way, q * 6 + a * 3 + c] = half[a][c][q].astype(BF16)
        for a in range(4):
            for c in range(3):
                for q in range(2):
                    ef[z, q * 12 + a * 3 + c] = both[a][c][q]
                    e2[z, q * 12 + a * 3 + c] = both[a][c][q].astype(BF16)

    for z in range(ZL):
        prepare(z)
        if z == 0:
            pl.semaphore_wait(barrier, 2 + 31 + 7)
            z_copy(0).start()
        for way in range(2):
            t_copy(way, z).start()
    z_copy(1).start()

    loads[1].wait()
    phase_tables(t, s, momenta_ref[...], cos_ref, sin_ref)
    total_ref[...] = jnp.zeros_like(total_ref)

    def even_step(z, carry):
        meson_part(e2, 0, z, cos_ref, sin_ref, total_ref)
        return carry

    lax.fori_loop(0, ZL, even_step, 0)
    loads[2].wait()

    def widen_links(i, carry):
        rows = pl.ds(pl.multiple_of(i * 96, 96), 96)
        lf[rows, :] = links_ref[rows, :].astype(F32)
        return carry

    lax.fori_loop(0, 6, widen_links, 0)

    def z_halves(i, carry):
        z, g = i // 2, lax.rem(i, 2)
        rows = pl.ds(pl.multiple_of(g * 8, 8), 8)
        for way, sign, source, target in ((0, -1, z + 1, z), (1, 1, z, z + 1)):
            half = project(load_spin(lambda comp: ef[source, comp, rows, :]), 2, sign)
            for a in range(2):
                for c in range(3):
                    for q in range(2):
                        zf[way, target, q * 6 + a * 3 + c, rows, :] = half[a][c][q]
        return carry

    lax.fori_loop(0, 2 * (ZL - 1), z_halves, 0)
    for way in range(2):
        z_copy(way).wait_recv()
    zf[0, ZL - 1] = hz[0].astype(F32)
    zf[1, 0] = hz[1].astype(F32)
    lane = lax.broadcasted_iota(jnp.int32, (8, 128), 1)
    first, last = (lane & 7) == 0, (lane & 7) == 7

    def link(way, d, z):
        def load(q, a, b):
            row = ((((way * 4 + d) * 2 + q) * 3 + a) * 3 + b) * ZL
            return lf[pl.ds(row + z, 1), :]

        return load

    def stored(read):
        return [[(read(a * 3 + c), read(6 + a * 3 + c)) for c in range(3)] for a in range(2)]

    def near_step(i, carry):
        z, g = i // 2, lax.rem(i, 2)
        rows = pl.ds(pl.multiple_of(g * 8, 8), 8)
        shifted = ((t + s * ZL + z + (lane >> 3) + 1) & 1) == 1
        spin = load_spin(lambda comp: ef[z, comp, rows, :])
        zero = jnp.zeros((8, 128), F32)
        total = [[(zero, zero) for _ in range(3)] for _ in range(4)]

        def x_ahead(v):
            ahead = jnp.where(last, pltpu.roll(v, 7, 1), pltpu.roll(v, 127, 1))
            return jnp.where(shifted, ahead, v)

        def x_behind(v):
            behind = jnp.where(first, pltpu.roll(v, 121, 1), pltpu.roll(v, 1, 1))
            return jnp.where(shifted, v, behind)

        for way, sign in ((0, -1), (1, 1)):
            for d in range(3):
                if d == 0:
                    half = map_half(project(spin, 0, sign), (x_ahead, x_behind)[way])
                elif d == 1:
                    half = map_half(
                        project(spin, 1, sign), lambda v: pltpu.roll(v, (120, 8)[way], 1)
                    )
                else:
                    half = stored(lambda comp: zf[way, z, comp, rows, :])
                total = add_hop(total, link_times(link(way, d, z), half, way == 1), d, sign)
        for a in range(4):
            for c in range(3):
                for q in range(2):
                    of[z, q * 12 + a * 3 + c, rows, :] = total[a][c][q]
        return carry

    lax.fori_loop(0, 2 * ZL, near_step, 0)
    loads[3].wait()

    def far_step(z, carry):
        for way in range(2):
            t_copy(way, z).wait_recv()
            tf[way] = ht[way, z].astype(F32)

        def group_step(g, carry):
            rows = pl.ds(pl.multiple_of(g * 8, 8), 8)
            total = load_spin(lambda comp: of[z, comp, rows, :])
            for way, sign in ((0, -1), (1, 1)):
                half = stored(lambda comp: tf[way, comp, rows, :])
                total = add_hop(total, link_times(link(way, 3, z), half, way == 1), 3, sign)
            for chir in range(2):
                source = [
                    tuple(hop_kappa * total[2 * chir + col // 3][col % 3][q] for q in range(2))
                    for col in range(6)
                ]
                for r in range(6):
                    out_real = out_imag = None
                    for col in range(6):
                        row = ((chir * 2 * 6 + r) * 6 + col) * ZL
                        cr = clover_ref[pl.ds(row + z, 1), :]
                        ci = clover_ref[pl.ds(row + 36 * ZL + z, 1), :]
                        vr, vi = source[col]
                        re, im = cr * vr - ci * vi, cr * vi + ci * vr
                        out_real = re if out_real is None else out_real + re
                        out_imag = im if out_imag is None else out_imag + im
                    place = 6 * chir + r
                    of[z, place, rows, :] = out_real
                    of[z, 12 + place, rows, :] = out_imag
            return carry

        lax.fori_loop(0, 2, group_step, 0)
        ob[z] = of[z].astype(BF16)
        meson_part(ob, 1, z, cos_ref, sin_ref, total_ref)
        return carry

    lax.fori_loop(0, ZL, far_step, 0)

    def send(stage, source, target, slot, device):
        pltpu.make_async_remote_copy(
            src_ref=source,
            dst_ref=target.at[slot],
            send_sem=x_send.at[stage],
            recv_sem=x_recv.at[stage],
            device_id=device,
            device_id_type=MESH,
        ).start()

    def wait(stage, target, count, sems):
        others = target.at[pl.ds(0, count)]
        pltpu.make_async_copy(others, others, sems.at[stage]).wait()

    def rows_of(index):
        return pl.ds(pl.multiple_of(index * 8, 8), 8)

    for step in plane_steps:
        device = in_plane(step)
        send(0, total_ref.at[rows_of(lax.rem(device[0], 8) * 4 + device[1])], arr1, place, device)
    arr1[place] = total_ref[rows_of(place), :]

    def turn(comp, carry):
        for z in range(ZL):
            for g in range(2):
                lf[pl.ds(g * 32 + z, 8, stride=4), :] = of[z, comp, pl.ds(g * 8, 8), :]
        odd_ref[:, comp] = lf[pl.ds(0, 64), :].astype(BF16).reshape(NMODE, ZL, 128)
        return carry

    lax.fori_loop(0, 24, turn, 0)
    loads[4].wait()
    loads[5].wait()
    weights = weights_ref[...]
    lane16 = lax.broadcasted_iota(jnp.int32, (NMODE, 128), 1)
    spread = (lane16 % NMODE == lax.broadcasted_iota(jnp.int32, (NMODE, 128), 0)).astype(F32)
    weight_j = jnp.dot(weights, spread, precision=lax.Precision.HIGHEST, preferred_element_type=F32)
    mode = lax.broadcasted_iota(jnp.int32, (1, NMODE), 1)
    pair_weights = [
        jnp.sum(
            jnp.where(mode == lax.rem(place, 2) * 8 + r, weights, 0.0), axis=1, keepdims=True
        )
        * weight_j
        for r in range(8)
    ]
    across = lax.broadcasted_iota(jnp.int32, (16, 16), 1)
    diagonal = across == lax.broadcasted_iota(jnp.int32, (16, 16), 0)
    separation = jnp.sum(
        jnp.where(diagonal, sep_ref[...].astype(F32), 0.0), axis=1, keepdims=True
    ).astype(jnp.int32)
    chosen = lax.broadcasted_iota(jnp.int32, (16, 128), 1) == lax.rem(t + separation, nt)
    wait(0, arr1, 31, x_recv)
    for j in range(8):
        field = arr1[4 * j] + arr1[4 * j + 1] + arr1[4 * j + 2] + arr1[4 * j + 3]
        turn2[pl.ds(j, 8, stride=8), :] = field
    send2[...] = turn2[...].astype(BF16)
    for step in ring_steps:
        send(1, send2, arr2, tz, along_planes(step))
    arr2[tz] = send2[...]
    own = send2[...].astype(F32)
    weighted = [own[8 * r : 8 * r + 8] * pair_weights[r] for r in range(8)]
    high = [v.astype(BF16) for v in weighted]
    low = [(v - h.astype(F32)).astype(BF16) for v, h in zip(weighted, high)]
    sources = jnp.concatenate(
        [jnp.concatenate(high, axis=1), jnp.concatenate(low, axis=1)], axis=0
    )
    wait(1, arr2, 7, x_recv)
    planes = [arr2[i].astype(F32) for i in range(8)]
    sinks = jnp.concatenate(
        [
            jnp.concatenate([planes[i][8 * r : 8 * r + 8] for i in range(8)], axis=0).astype(BF16)
            for r in range(8)
        ],
        axis=1,
    )
    sinks = jnp.concatenate([sinks, sinks], axis=0)
    product = lax.dot_general(
        sources, sinks, (((1,), (1,)), ((), ())), preferred_element_type=F32
    )
    gathered[...] = product[:8] + product[8:]
    for j in range(8):
        send3[j] = gathered[pl.ds(j, 1), :]
    for step in plane_steps:
        device = in_plane(step)
        send(2, send3.at[lax.rem(device[0], 8)], arr3, place, device)
    arr3[place] = send3[lax.rem(t, 8)]
    wait(2, arr3, 31, x_recv)
    row = jnp.sum(arr3[...], axis=0)
    picked = jnp.sum(jnp.where(chosen, row, 0.0), axis=1, keepdims=True)
    out_ref[...] = jnp.sum(jnp.where(diagonal, picked, 0.0), axis=0, keepdims=True) * (
        1.0 / (16.0 * NMODE * NMOM * LS**3)
    )
    for way in range(2):
        z_copy(way).wait_send()
        for z in range(ZL):
            t_copy(way, z).wait_send()
    for stage, target, count in ((0, arr1, 31), (1, arr2, 7), (2, arr3, 31)):
        wait(stage, target, count, x_send)


def body(nt, ns, even_modes, hop_links, clover_inverse, momenta, mode_weights, separations):
    vmem = pl.BlockSpec(memory_space=pltpu.VMEM)
    hbm = pl.BlockSpec(memory_space=pltpu.HBM)
    shape = jax.ShapeDtypeStruct
    dma = pltpu.SemaphoreType.DMA
    sites = (ZL, 24, NMODE, 128)
    odd_modes, correlator = pl.pallas_call(
        functools.partial(kernel, nt, ns),
        out_shape=(shape((NMODE, 24, ZL, 128), BF16), shape((1, 16), F32)),
        in_specs=[hbm] * 6,
        out_specs=(vmem, vmem),
        scratch_shapes=[
            pltpu.VMEM((NMODE * 24 * ZL, 128), BF16),
            pltpu.VMEM((144 * ZL, 128), BF16),
            pltpu.VMEM((144 * ZL, 128), F32),
            pltpu.VMEM((3, NMOM), jnp.int32),
            pltpu.VMEM((1, NMODE), F32),
            pltpu.VMEM((1, 16), jnp.int32),
            pltpu.VMEM(sites, F32),
            pltpu.VMEM((NMODE * 24 * ZL, 128), F32),
            pltpu.VMEM(sites, BF16),
            pltpu.VMEM((2, ZL, 12, NMODE, 128), BF16),
            pltpu.VMEM((2, 12, NMODE, 128), BF16),
            pltpu.VMEM((2, ZL, 12, NMODE, 128), BF16),
            pltpu.VMEM((2, 12, NMODE, 128), BF16),
            pltpu.VMEM((2, 12, NMODE, 128), F32),
            pltpu.VMEM((2, ZL, 12, NMODE, 128), F32),
            pltpu.VMEM((144 * ZL, 128), F32),
            pltpu.VMEM(sites, F32),
            pltpu.VMEM(sites, BF16),
            pltpu.VMEM((2, ZL, NMOM, 128), F32),
            pltpu.VMEM((2, ZL, NMOM, 128), F32),
            pltpu.VMEM((NMOM * NMODE, 128), F32),
            pltpu.VMEM((32, 8, 128), F32),
            pltpu.VMEM((64, 128), F32),
            pltpu.VMEM((64, 128), BF16),
            pltpu.VMEM((8, 64, 128), BF16),
            pltpu.VMEM((8, 128), F32),
            pltpu.VMEM((8, 1, 128), F32),
            pltpu.VMEM((32, 1, 128), F32),
            dma((6,)), dma((2, ZL)), dma((2, ZL)), dma((2,)), dma((2,)), dma((3,)), dma((3,)),
        ],
        compiler_params=pltpu.CompilerParams(
            collective_id=0, has_side_effects=True, vmem_limit_bytes=63 * 1024 * 1024
        ),
        name="correlator",
    )(
        even_modes.reshape(NMODE * 24 * ZL, 128),
        hop_links.reshape(144 * ZL, 128),
        clover_inverse.reshape(144 * ZL, 128),
        momenta.T,
        mode_weights.reshape(1, NMODE),
        separations,
    )
    return odd_modes.reshape(even_modes.shape), correlator


def solution(mesh):
    in_specs = (
        P(None, None, None, None, "ta", "sa", None),
        P(None, None, None, None, None, "ta", "sa", None),
        P(None, None, None, None, "ta", "sa", None),
        P(),
        P(),
        P("ta", None),
    )
    out_specs = (P(None, None, None, None, "ta", "sa", None), P("ta", None))
    return jax.shard_map(
        functools.partial(body, mesh.shape["ta"], mesh.shape["sa"]),
        mesh=mesh,
        in_specs=in_specs,
        out_specs=out_specs,
        check_vma=False,
    )
```

```python
import functools
import math

import jax
import jax.numpy as jnp
from jax import lax
from jax.experimental import pallas as pl
from jax.experimental.pallas import tpu as pltpu
from jax.sharding import PartitionSpec as P

NMODE = 16
NMOM = 16
LS = 16
ZL = 4
F32 = jnp.float32
BF16 = jnp.bfloat16
MESH = pl.DeviceIdType.MESH

hop_kappa = 0.125
gamma_source = ((3, 2, 1, 0), (3, 2, 1, 0), (2, 3, 0, 1), (2, 3, 0, 1))
gamma_factor = ((3, 3, 2, 2), (1, 0, 0, 1), (3, 2, 2, 3), (0, 0, 0, 0))
factor_parts = ((1, 0), (-1, 0), (0, 1), (0, -1))


def add_factor(base, value, code, sign):
    (br, bi), (vr, vi) = base, value
    re, im = factor_parts[code]
    re, im = re * sign, im * sign
    if re == 1:
        return br + vr, bi + vi
    if re == -1:
        return br - vr, bi - vi
    if im == 1:
        return br - vi, bi + vr
    return br + vi, bi - vr


def project(spin, d, sign):
    return [
        [
            add_factor(spin[s][c], spin[gamma_source[d][s]][c], gamma_factor[d][s], sign)
            for c in range(3)
        ]
        for s in range(2)
    ]


def load_spin(load):
    return [[(load(s * 3 + c), load(12 + s * 3 + c)) for c in range(3)] for s in range(4)]


def link_times(load, half, adjoint):
    out = [[None] * 3 for _ in range(2)]
    for a in range(3):
        for b in range(3):
            lr, li = (load(0, b, a), load(1, b, a)) if adjoint else (load(0, a, b), load(1, a, b))
            for s in range(2):
                hr, hi = half[s][b]
                if adjoint:
                    re, im = lr * hr + li * hi, lr * hi - li * hr
                else:
                    re, im = lr * hr - li * hi, lr * hi + li * hr
                old = out[s][a]
                out[s][a] = (re, im) if old is None else (old[0] + re, old[1] + im)
    return out


def add_hop(total, half, d, sign):
    for s in range(2):
        for c in range(3):
            total[s][c] = (total[s][c][0] + half[s][c][0], total[s][c][1] + half[s][c][1])
    for s in range(2, 4):
        for c in range(3):
            total[s][c] = add_factor(
                total[s][c], half[gamma_source[d][s]][c], gamma_factor[d][s], sign
            )
    return total


def map_half(half, f):
    return [[(f(half[s][c][0]), f(half[s][c][1])) for c in range(3)] for s in range(2)]


def circle(step):
    fold = jnp.where(step > 8, 16 - step, step)
    low = jnp.where(fold > 4, 8 - fold, fold)
    value = jnp.where(low == 1, math.cos(math.pi / 8), 1.0).astype(F32)
    value = jnp.where(low == 2, math.cos(math.pi / 4), value).astype(F32)
    value = jnp.where(low == 3, math.cos(3 * math.pi / 8), value).astype(F32)
    value = jnp.where(low == 4, 0.0, value).astype(F32)
    return jnp.where(fold > 4, -value, value)


def phase_tables(t, s, momenta, cos_ref, sin_ref):
    lane = lax.broadcasted_iota(jnp.int32, (NMOM, 128), 1)
    y, h = lane >> 3, lane & 7
    place = lax.broadcasted_iota(jnp.int32, (NMOM, NMOM), 1)
    diagonal = place == lax.broadcasted_iota(jnp.int32, (NMOM, NMOM), 0)
    nx, ny, nz = (
        jnp.sum(
            jnp.where(diagonal, momenta[d : d + 1, :].astype(F32), 0.0), axis=1, keepdims=True
        ).astype(jnp.int32)
        for d in range(3)
    )
    for parity in range(2):
        for zl in range(ZL):
            z = s * ZL + zl
            x = 2 * h + ((t + z + y + parity) & 1)
            step = (nx * x + ny * y + nz * z) & 15
            cos_ref[parity, zl] = circle(step)
            sin_ref[parity, zl] = circle((step + 12) & 15)


def meson_part(modes_ref, parity, z, cos_ref, sin_ref, total_ref):
    for a in range(4):
        for c in range(3):
            comp = a * 3 + c
            vr = modes_ref[z, comp].astype(F32)
            vi = modes_ref[z, 12 + comp].astype(F32)
            rows = []
            for p in range(NMOM):
                cs = cos_ref[parity, z, pl.ds(p, 1), :]
                sn = sin_ref[parity, z, pl.ds(p, 1), :]
                rows.append(
                    jnp.concatenate(
                        [
                            (vr * cs - vi * sn).astype(BF16),
                            (-(vr * sn + vi * cs)).astype(BF16),
                        ],
                        axis=1,
                    )
                )
            left = jnp.concatenate(rows, axis=0)
            real_rows, imag_rows = [], []
            for k in range(4):
                other = gamma_source[k][a] * 3 + c
                wr = modes_ref[z, other]
                wi = modes_ref[z, 12 + other]
                re, im = factor_parts[gamma_factor[k][a]]
                if re == 1:
                    gr, gi = wr, wi
                elif re == -1:
                    gr, gi = -wr, -wi
                elif im == 1:
                    gr, gi = -wi, wr
                else:
                    gr, gi = wi, -wr
                real_rows.append(jnp.concatenate([gr, -gi], axis=1))
                imag_rows.append(jnp.concatenate([gi, gr], axis=1))
            right = jnp.concatenate(real_rows + imag_rows, axis=0)
            total_ref[...] += lax.dot_general(
                left, right, (((1,), (1,)), ((), ())), preferred_element_type=F32
            )


def plane_distance(step):
    dy, dx, dn, dc = step
    return -(min(dy, 4 - dy) + (2 * dx if not dn else 1)), -dc


plane_steps = sorted(
    [
        (dy, dx, dn, dc)
        for dy in range(4)
        for dx in range(2)
        for dn in range(2)
        for dc in range(2)
        if dy or dx or dn or dc
    ],
    key=plane_distance,
)
ring_steps = (4, 3, 5, 2, 6, 1, 7)


def kernel(
    nt, ns,
    e_hbm, links_hbm, clover_hbm, momenta_hbm, weights_hbm, sep_hbm,
    odd_ref, out_ref,
    e_ref, links_ref, clover_ref, momenta_ref, weights_ref, sep_ref,
    ef, ewide, e2, st, sz, ht, hz, tf, zf, lf, of, ob, cos_ref, sin_ref,
    total_ref, arr1, turn2, send2, arr2, gathered, send3, arr3,
    in_sem, ts_sem, tr_sem, zs_sem, zr_sem, x_send, x_recv,
):
    t = lax.axis_index("ta")
    s = lax.axis_index("sa")
    tz, ty, tx = t // 8, lax.rem(t, 8) // 2, lax.rem(t, 2)
    t_up, t_dn = lax.rem(t + 1, nt), lax.rem(t + nt - 1, nt)
    s_up, s_dn = lax.rem(s + 1, ns), lax.rem(s + ns - 1, ns)
    partners = ((t_dn, s), (t_up, s), (t, s_dn), (t, s_up))
    place = lax.rem(t, 8) * 4 + s

    def in_plane(step):
        dy, dx, dn, dc = step
        x_half, x_near, core = lax.rem(tx + dx, 2), lax.rem(s // 2 + dn, 2), lax.rem(s + dc, 2)
        return tz * 8 + lax.rem(ty + dy, 4) * 2 + x_half, x_near * 2 + core

    def along_planes(step):
        return lax.rem(tz + step, 8) * 8 + lax.rem(t, 8), s

    loads = []
    for i, (source, target) in enumerate(
        (
            (e_hbm, e_ref), (momenta_hbm, momenta_ref), (links_hbm, links_ref),
            (clover_hbm, clover_ref), (weights_hbm, weights_ref), (sep_hbm, sep_ref),
        )
    ):
        load = pltpu.make_async_copy(source, target, in_sem.at[i])
        load.start()
        loads.append(load)
    barrier = pltpu.get_barrier_semaphore()
    for partner in partners[:2]:
        pl.semaphore_signal(barrier, inc=1, device_id=partner, device_id_type=MESH)
    for step in plane_steps:
        pl.semaphore_signal(barrier, inc=1, device_id=in_plane(step), device_id_type=MESH)
    for step in ring_steps:
        pl.semaphore_signal(barrier, inc=1, device_id=along_planes(step), device_id_type=MESH)

    loads[0].wait()

    def widen(m, carry):
        rows = pl.ds(pl.multiple_of(m * 96, 96), 96)
        ewide[rows, :] = e_ref[rows, :].astype(F32)
        return carry

    lax.fori_loop(0, NMODE, widen, 0)
    sign_dn = jnp.where(t == 0, -1.0, 1.0).astype(F32)
    sign_up = jnp.where(t == nt - 1, -1.0, 1.0).astype(F32)

    def t_copy(way, z):
        return pltpu.make_async_remote_copy(
            src_ref=st.at[way, z],
            dst_ref=ht.at[way, z],
            send_sem=ts_sem.at[way, z],
            recv_sem=tr_sem.at[way, z],
            device_id=partners[way],
            device_id_type=MESH,
        )

    def z_copy(way):
        return pltpu.make_async_remote_copy(
            src_ref=sz.at[way],
            dst_ref=hz.at[way],
            send_sem=zs_sem.at[way],
            recv_sem=zr_sem.at[way],
            device_id=partners[2 + way],
            device_id_type=MESH,
        )

    def prepare(z):
        halves = []
        for g in range(2):
            halves.append(
                load_spin(
                    lambda comp: ewide[pl.ds((g * 8 * 24 + comp) * 4 + z, 8, stride=96), :]
                )
            )
        both = [
            [
                tuple(
                    jnp.concatenate([halves[0][a][c][q], halves[1][a][c][q]], axis=0)
                    for q in range(2)
                )
                for c in range(3)
            ]
            for a in range(4)
        ]
        for way, sign, factor in ((0, -1, sign_dn), (1, 1, sign_up)):
            half = project(both, 3, sign)
            for a in range(2):
                for c in range(3):
                    for q in range(2):
                        st[way, z, q * 6 + a * 3 + c] = (half[a][c][q] * factor).astype(BF16)
        for edge, way, sign in ((0, 0, -1), (ZL - 1, 1, 1)):
            if z == edge:
                half = project(both, 2, sign)
                for a in range(2):
                    for c in range(3):
                        for q in range(2):
                            sz[way, q * 6 + a * 3 + c] = half[a][c][q].astype(BF16)
        for a in range(4):
            for c in range(3):
                for q in range(2):
                    ef[z, q * 12 + a * 3 + c] = both[a][c][q]
                    e2[z, q * 12 + a * 3 + c] = both[a][c][q].astype(BF16)

    for z in (0, 3, 2, 1):
        prepare(z)
        if z == 0:
            pl.semaphore_wait(barrier, 2 + 31 + 7)
            z_copy(0).start()
        if z == ZL - 1:
            z_copy(1).start()
        for way in range(2):
            t_copy(way, z).start()

    loads[1].wait()
    phase_tables(t, s, momenta_ref[...], cos_ref, sin_ref)
    total_ref[...] = jnp.zeros_like(total_ref)

    def even_step(z, carry):
        meson_part(e2, 0, z, cos_ref, sin_ref, total_ref)
        return carry

    lax.fori_loop(0, ZL, even_step, 0)
    loads[2].wait()

    def widen_links(i, carry):
        rows = pl.ds(pl.multiple_of(i * 96, 96), 96)
        lf[rows, :] = links_ref[rows, :].astype(F32)
        return carry

    lax.fori_loop(0, 6, widen_links, 0)

    def z_halves(i, carry):
        z, g = i // 2, lax.rem(i, 2)
        rows = pl.ds(pl.multiple_of(g * 8, 8), 8)
        for way, sign, source, target in ((0, -1, z + 1, z), (1, 1, z, z + 1)):
            half = project(load_spin(lambda comp: ef[source, comp, rows, :]), 2, sign)
            for a in range(2):
                for c in range(3):
                    for q in range(2):
                        zf[way, target, q * 6 + a * 3 + c, rows, :] = half[a][c][q]
        return carry

    lax.fori_loop(0, 2 * (ZL - 1), z_halves, 0)
    for way in range(2):
        z_copy(way).wait_recv()
    zf[0, ZL - 1] = hz[0].astype(F32)
    zf[1, 0] = hz[1].astype(F32)
    lane = lax.broadcasted_iota(jnp.int32, (8, 128), 1)
    first, last = (lane & 7) == 0, (lane & 7) == 7

    def link(way, d, z):
        def load(q, a, b):
            row = ((((way * 4 + d) * 2 + q) * 3 + a) * 3 + b) * ZL
            return lf[pl.ds(row + z, 1), :]

        return load

    def stored(read):
        return [[(read(a * 3 + c), read(6 + a * 3 + c)) for c in range(3)] for a in range(2)]

    def near_step(i, carry):
        z, g = i // 2, lax.rem(i, 2)
        rows = pl.ds(pl.multiple_of(g * 8, 8), 8)
        shifted = ((t + s * ZL + z + (lane >> 3) + 1) & 1) == 1
        spin = load_spin(lambda comp: ef[z, comp, rows, :])
        zero = jnp.zeros((8, 128), F32)
        total = [[(zero, zero) for _ in range(3)] for _ in range(4)]

        def x_ahead(v):
            ahead = jnp.where(last, pltpu.roll(v, 7, 1), pltpu.roll(v, 127, 1))
            return jnp.where(shifted, ahead, v)

        def x_behind(v):
            behind = jnp.where(first, pltpu.roll(v, 121, 1), pltpu.roll(v, 1, 1))
            return jnp.where(shifted, v, behind)

        for way, sign in ((0, -1), (1, 1)):
            for d in range(3):
                if d == 0:
                    half = map_half(project(spin, 0, sign), (x_ahead, x_behind)[way])
                elif d == 1:
                    half = map_half(
                        project(spin, 1, sign), lambda v: pltpu.roll(v, (120, 8)[way], 1)
                    )
                else:
                    half = stored(lambda comp: zf[way, z, comp, rows, :])
                total = add_hop(total, link_times(link(way, d, z), half, way == 1), d, sign)
        for a in range(4):
            for c in range(3):
                for q in range(2):
                    of[z, q * 12 + a * 3 + c, rows, :] = total[a][c][q]
        return carry

    lax.fori_loop(0, 2 * ZL, near_step, 0)
    loads[3].wait()

    def far_step(i, carry):
        z = lax.rem(3 * i, ZL)
        for way in range(2):
            t_copy(way, z).wait_recv()
            tf[way] = ht[way, z].astype(F32)

        def group_step(g, carry):
            rows = pl.ds(pl.multiple_of(g * 8, 8), 8)
            total = load_spin(lambda comp: of[z, comp, rows, :])
            for way, sign in ((0, -1), (1, 1)):
                half = stored(lambda comp: tf[way, comp, rows, :])
                total = add_hop(total, link_times(link(way, 3, z), half, way == 1), 3, sign)
            for chir in range(2):
                source = [
                    tuple(hop_kappa * total[2 * chir + col // 3][col % 3][q] for q in range(2))
                    for col in range(6)
                ]
                for r in range(6):
                    out_real = out_imag = None
                    for col in range(6):
                        row = ((chir * 2 * 6 + r) * 6 + col) * ZL
                        cr = clover_ref[pl.ds(row + z, 1), :]
                        ci = clover_ref[pl.ds(row + 36 * ZL + z, 1), :]
                        vr, vi = source[col]
                        re, im = cr * vr - ci * vi, cr * vi + ci * vr
                        out_real = re if out_real is None else out_real + re
                        out_imag = im if out_imag is None else out_imag + im
                    place = 6 * chir + r
                    of[z, place, rows, :] = out_real
                    of[z, 12 + place, rows, :] = out_imag
            return carry

        lax.fori_loop(0, 2, group_step, 0)
        ob[z] = of[z].astype(BF16)
        meson_part(ob, 1, z, cos_ref, sin_ref, total_ref)
        return carry

    lax.fori_loop(0, ZL, far_step, 0)

    def send(stage, source, target, slot, device):
        pltpu.make_async_remote_copy(
            src_ref=source,
            dst_ref=target.at[slot],
            send_sem=x_send.at[stage],
            recv_sem=x_recv.at[stage],
            device_id=device,
            device_id_type=MESH,
        ).start()

    def wait(stage, target, count, sems):
        others = target.at[pl.ds(0, count)]
        pltpu.make_async_copy(others, others, sems.at[stage]).wait()

    def rows_of(index):
        return pl.ds(pl.multiple_of(index * 8, 8), 8)

    for step in plane_steps:
        device = in_plane(step)
        send(0, total_ref.at[rows_of(lax.rem(device[0], 8) * 4 + device[1])], arr1, place, device)
    arr1[place] = total_ref[rows_of(place), :]

    def turn(comp, carry):
        for z in range(ZL):
            for g in range(2):
                lf[pl.ds(g * 32 + z, 8, stride=4), :] = of[z, comp, pl.ds(g * 8, 8), :]
        odd_ref[:, comp] = lf[pl.ds(0, 64), :].astype(BF16).reshape(NMODE, ZL, 128)
        return carry

    lax.fori_loop(0, 24, turn, 0)
    loads[4].wait()
    loads[5].wait()
    weights = weights_ref[...]
    lane16 = lax.broadcasted_iota(jnp.int32, (NMODE, 128), 1)
    spread = (lane16 % NMODE == lax.broadcasted_iota(jnp.int32, (NMODE, 128), 0)).astype(F32)
    weight_j = jnp.dot(weights, spread, precision=lax.Precision.HIGHEST, preferred_element_type=F32)
    mode = lax.broadcasted_iota(jnp.int32, (1, NMODE), 1)
    pair_weights = [
        jnp.sum(
            jnp.where(mode == lax.rem(place, 2) * 8 + r, weights, 0.0), axis=1, keepdims=True
        )
        * weight_j
        for r in range(8)
    ]
    across = lax.broadcasted_iota(jnp.int32, (16, 16), 1)
    diagonal = across == lax.broadcasted_iota(jnp.int32, (16, 16), 0)
    separation = jnp.sum(
        jnp.where(diagonal, sep_ref[...].astype(F32), 0.0), axis=1, keepdims=True
    ).astype(jnp.int32)
    chosen = lax.broadcasted_iota(jnp.int32, (16, 128), 1) == lax.rem(t + separation, nt)
    wait(0, arr1, 31, x_recv)
    for j in range(8):
        field = arr1[4 * j] + arr1[4 * j + 1] + arr1[4 * j + 2] + arr1[4 * j + 3]
        turn2[pl.ds(j, 8, stride=8), :] = field
    send2[...] = turn2[...].astype(BF16)
    for step in ring_steps:
        send(1, send2, arr2, tz, along_planes(step))
    arr2[tz] = send2[...]
    own = send2[...].astype(F32)
    weighted = [own[8 * r : 8 * r + 8] * pair_weights[r] for r in range(8)]
    high = [v.astype(BF16) for v in weighted]
    low = [(v - h.astype(F32)).astype(BF16) for v, h in zip(weighted, high)]
    sources = jnp.concatenate(
        [jnp.concatenate(high, axis=1), jnp.concatenate(low, axis=1)], axis=0
    )
    wait(1, arr2, 7, x_recv)
    planes = [arr2[i].astype(F32) for i in range(8)]
    sinks = jnp.concatenate(
        [
            jnp.concatenate([planes[i][8 * r : 8 * r + 8] for i in range(8)], axis=0).astype(BF16)
            for r in range(8)
        ],
        axis=1,
    )
    sinks = jnp.concatenate([sinks, sinks], axis=0)
    product = lax.dot_general(
        sources, sinks, (((1,), (1,)), ((), ())), preferred_element_type=F32
    )
    gathered[...] = product[:8] + product[8:]
    for j in range(8):
        send3[j] = gathered[pl.ds(j, 1), :]
    for step in plane_steps:
        device = in_plane(step)
        send(2, send3.at[lax.rem(device[0], 8)], arr3, place, device)
    arr3[place] = send3[lax.rem(t, 8)]
    wait(2, arr3, 31, x_recv)
    row = jnp.sum(arr3[...], axis=0)
    picked = jnp.sum(jnp.where(chosen, row, 0.0), axis=1, keepdims=True)
    out_ref[...] = jnp.sum(jnp.where(diagonal, picked, 0.0), axis=0, keepdims=True) * (
        1.0 / (16.0 * NMODE * NMOM * LS**3)
    )
    for way in range(2):
        z_copy(way).wait_send()
        for z in range(ZL):
            t_copy(way, z).wait_send()
    for stage, target, count in ((0, arr1, 31), (1, arr2, 7), (2, arr3, 31)):
        wait(stage, target, count, x_send)


def body(nt, ns, even_modes, hop_links, clover_inverse, momenta, mode_weights, separations):
    vmem = pl.BlockSpec(memory_space=pltpu.VMEM)
    hbm = pl.BlockSpec(memory_space=pltpu.HBM)
    shape = jax.ShapeDtypeStruct
    dma = pltpu.SemaphoreType.DMA
    sites = (ZL, 24, NMODE, 128)
    odd_modes, correlator = pl.pallas_call(
        functools.partial(kernel, nt, ns),
        out_shape=(pltpu.VMEM((NMODE, 24, ZL, 128), BF16), pltpu.VMEM((1, 16), F32)),
        in_specs=[hbm] * 6,
        out_specs=(vmem, vmem),
        scratch_shapes=[
            pltpu.VMEM((NMODE * 24 * ZL, 128), BF16),
            pltpu.VMEM((144 * ZL, 128), BF16),
            pltpu.VMEM((144 * ZL, 128), F32),
            pltpu.VMEM((3, NMOM), jnp.int32),
            pltpu.VMEM((1, NMODE), F32),
            pltpu.VMEM((1, 16), jnp.int32),
            pltpu.VMEM(sites, F32),
            pltpu.VMEM((NMODE * 24 * ZL, 128), F32),
            pltpu.VMEM(sites, BF16),
            pltpu.VMEM((2, ZL, 12, NMODE, 128), BF16),
            pltpu.VMEM((2, 12, NMODE, 128), BF16),
            pltpu.VMEM((2, ZL, 12, NMODE, 128), BF16),
            pltpu.VMEM((2, 12, NMODE, 128), BF16),
            pltpu.VMEM((2, 12, NMODE, 128), F32),
            pltpu.VMEM((2, ZL, 12, NMODE, 128), F32),
            pltpu.VMEM((144 * ZL, 128), F32),
            pltpu.VMEM(sites, F32),
            pltpu.VMEM(sites, BF16),
            pltpu.VMEM((2, ZL, NMOM, 128), F32),
            pltpu.VMEM((2, ZL, NMOM, 128), F32),
            pltpu.VMEM((NMOM * NMODE, 128), F32),
            pltpu.VMEM((32, 8, 128), F32),
            pltpu.VMEM((64, 128), F32),
            pltpu.VMEM((64, 128), BF16),
            pltpu.VMEM((8, 64, 128), BF16),
            pltpu.VMEM((8, 128), F32),
            pltpu.VMEM((8, 1, 128), F32),
            pltpu.VMEM((32, 1, 128), F32),
            dma((6,)), dma((2, ZL)), dma((2, ZL)), dma((2,)), dma((2,)), dma((3,)), dma((3,)),
        ],
        compiler_params=pltpu.CompilerParams(
            collective_id=0, has_side_effects=True, vmem_limit_bytes=63 * 1024 * 1024
        ),
        name="correlator",
    )(
        even_modes.reshape(NMODE * 24 * ZL, 128),
        hop_links.reshape(144 * ZL, 128),
        clover_inverse.reshape(144 * ZL, 128),
        momenta.T,
        mode_weights.reshape(1, NMODE),
        separations,
    )
    return odd_modes.reshape(even_modes.shape), correlator


def solution(mesh):
    in_specs = (
        P(None, None, None, None, "ta", "sa", None),
        P(None, None, None, None, None, "ta", "sa", None),
        P(None, None, None, None, "ta", "sa", None),
        P(),
        P(),
        P("ta", None),
    )
    out_specs = (P(None, None, None, None, "ta", "sa", None), P("ta", None))
    return jax.shard_map(
        functools.partial(body, mesh.shape["ta"], mesh.shape["sa"]),
        mesh=mesh,
        in_specs=in_specs,
        out_specs=out_specs,
        check_vma=False,
    )
```

```python
import functools
import math

import jax
import jax.numpy as jnp
from jax import lax
from jax.experimental import pallas as pl
from jax.experimental.pallas import tpu as pltpu
from jax.sharding import PartitionSpec as P

NMODE = 16
NMOM = 16
LS = 16
ZL = 4
F32 = jnp.float32
BF16 = jnp.bfloat16
MESH = pl.DeviceIdType.MESH

hop_kappa = 0.125
gamma_source = ((3, 2, 1, 0), (3, 2, 1, 0), (2, 3, 0, 1), (2, 3, 0, 1))
gamma_factor = ((3, 3, 2, 2), (1, 0, 0, 1), (3, 2, 2, 3), (0, 0, 0, 0))
factor_parts = ((1, 0), (-1, 0), (0, 1), (0, -1))


def add_factor(base, value, code, sign):
    (br, bi), (vr, vi) = base, value
    re, im = factor_parts[code]
    re, im = re * sign, im * sign
    if re == 1:
        return br + vr, bi + vi
    if re == -1:
        return br - vr, bi - vi
    if im == 1:
        return br - vi, bi + vr
    return br + vi, bi - vr


def project(spin, d, sign):
    return [
        [
            add_factor(spin[s][c], spin[gamma_source[d][s]][c], gamma_factor[d][s], sign)
            for c in range(3)
        ]
        for s in range(2)
    ]


def load_spin(load):
    return [[(load(s * 3 + c), load(12 + s * 3 + c)) for c in range(3)] for s in range(4)]


def link_times(load, half, adjoint):
    out = [[None] * 3 for _ in range(2)]
    for a in range(3):
        for b in range(3):
            lr, li = (load(0, b, a), load(1, b, a)) if adjoint else (load(0, a, b), load(1, a, b))
            for s in range(2):
                hr, hi = half[s][b]
                if adjoint:
                    re, im = lr * hr + li * hi, lr * hi - li * hr
                else:
                    re, im = lr * hr - li * hi, lr * hi + li * hr
                old = out[s][a]
                out[s][a] = (re, im) if old is None else (old[0] + re, old[1] + im)
    return out


def add_hop(total, half, d, sign):
    for s in range(2):
        for c in range(3):
            total[s][c] = (total[s][c][0] + half[s][c][0], total[s][c][1] + half[s][c][1])
    for s in range(2, 4):
        for c in range(3):
            total[s][c] = add_factor(
                total[s][c], half[gamma_source[d][s]][c], gamma_factor[d][s], sign
            )
    return total


def map_half(half, f):
    return [[(f(half[s][c][0]), f(half[s][c][1])) for c in range(3)] for s in range(2)]


def circle(step):
    fold = jnp.where(step > 8, 16 - step, step)
    low = jnp.where(fold > 4, 8 - fold, fold)
    value = jnp.where(low == 1, math.cos(math.pi / 8), 1.0).astype(F32)
    value = jnp.where(low == 2, math.cos(math.pi / 4), value).astype(F32)
    value = jnp.where(low == 3, math.cos(3 * math.pi / 8), value).astype(F32)
    value = jnp.where(low == 4, 0.0, value).astype(F32)
    return jnp.where(fold > 4, -value, value)


def phase_tables(t, s, momenta, cos_ref, sin_ref):
    lane = lax.broadcasted_iota(jnp.int32, (NMOM, 128), 1)
    y, h = lane >> 3, lane & 7
    place = lax.broadcasted_iota(jnp.int32, (NMOM, NMOM), 1)
    diagonal = place == lax.broadcasted_iota(jnp.int32, (NMOM, NMOM), 0)
    nx, ny, nz = (
        jnp.sum(
            jnp.where(diagonal, momenta[d : d + 1, :].astype(F32), 0.0), axis=1, keepdims=True
        ).astype(jnp.int32)
        for d in range(3)
    )
    for parity in range(2):
        for zl in range(ZL):
            z = s * ZL + zl
            x = 2 * h + ((t + z + y + parity) & 1)
            step = (nx * x + ny * y + nz * z) & 15
            cos_ref[parity, zl] = circle(step)
            sin_ref[parity, zl] = circle((step + 12) & 15)


def meson_part(modes_ref, parity, z, cos_ref, sin_ref, total_ref):
    for a in range(4):
        for c in range(3):
            comp = a * 3 + c
            vr = modes_ref[z, comp].astype(F32)
            vi = modes_ref[z, 12 + comp].astype(F32)
            rows = []
            for p in range(NMOM):
                cs = cos_ref[parity, z, pl.ds(p, 1), :]
                sn = sin_ref[parity, z, pl.ds(p, 1), :]
                rows.append(
                    jnp.concatenate(
                        [
                            (vr * cs - vi * sn).astype(BF16),
                            (-(vr * sn + vi * cs)).astype(BF16),
                        ],
                        axis=1,
                    )
                )
            left = jnp.concatenate(rows, axis=0)
            real_rows, imag_rows = [], []
            for k in range(4):
                other = gamma_source[k][a] * 3 + c
                wr = modes_ref[z, other]
                wi = modes_ref[z, 12 + other]
                re, im = factor_parts[gamma_factor[k][a]]
                if re == 1:
                    gr, gi = wr, wi
                elif re == -1:
                    gr, gi = -wr, -wi
                elif im == 1:
                    gr, gi = -wi, wr
                else:
                    gr, gi = wi, -wr
                real_rows.append(jnp.concatenate([gr, -gi], axis=1))
                imag_rows.append(jnp.concatenate([gi, gr], axis=1))
            right = jnp.concatenate(real_rows + imag_rows, axis=0)
            total_ref[...] += lax.dot_general(
                left, right, (((1,), (1,)), ((), ())), preferred_element_type=F32
            )


def plane_distance(step):
    dy, dx, dn, dc = step
    return -(min(dy, 4 - dy) + (2 * dx if not dn else 1)), -dc


plane_steps = sorted(
    [
        (dy, dx, dn, dc)
        for dy in range(4)
        for dx in range(2)
        for dn in range(2)
        for dc in range(2)
        if dy or dx or dn or dc
    ],
    key=plane_distance,
)
ring_steps = (4, 3, 5, 2, 6, 1, 7)


def kernel(
    nt, ns,
    e_hbm, links_hbm, clover_hbm, momenta_hbm, weights_hbm, sep_hbm,
    odd_ref, out_ref,
    e_ref, links_ref, clover_ref, momenta_ref, weights_ref, sep_ref,
    ef, ewide, e2, st, sz, ht, hz, tf, zf, lf, of, ob, cos_ref, sin_ref,
    total_ref, arr1, turn2, send2, arr2, gathered, send3, arr3,
    e_sem, in_sem, ts_sem, tr_sem, zs_sem, zr_sem, x_send, x_recv,
):
    t = lax.axis_index("ta")
    s = lax.axis_index("sa")
    tz, ty, tx = t // 8, lax.rem(t, 8) // 2, lax.rem(t, 2)
    t_up, t_dn = lax.rem(t + 1, nt), lax.rem(t + nt - 1, nt)
    s_up, s_dn = lax.rem(s + 1, ns), lax.rem(s + ns - 1, ns)
    partners = ((t_dn, s), (t_up, s), (t, s_dn), (t, s_up))
    place = lax.rem(t, 8) * 4 + s

    def in_plane(step):
        dy, dx, dn, dc = step
        x_half, x_near, core = lax.rem(tx + dx, 2), lax.rem(s // 2 + dn, 2), lax.rem(s + dc, 2)
        return tz * 8 + lax.rem(ty + dy, 4) * 2 + x_half, x_near * 2 + core

    def along_planes(step):
        return lax.rem(tz + step, 8) * 8 + lax.rem(t, 8), s

    loads = []
    e_loads = []
    for i in range(4):
        part = pl.ds(i * 384, 384)
        load = pltpu.make_async_copy(e_hbm.at[part], e_ref.at[part], e_sem.at[i])
        load.start()
        e_loads.append(load)
    for i, (source, target) in enumerate(
        (
            (momenta_hbm, momenta_ref), (links_hbm, links_ref), (clover_hbm, clover_ref),
            (weights_hbm, weights_ref), (sep_hbm, sep_ref),
        )
    ):
        load = pltpu.make_async_copy(source, target, in_sem.at[i])
        load.start()
        loads.append(load)
    barrier = pltpu.get_barrier_semaphore()
    for partner in partners[:2]:
        pl.semaphore_signal(barrier, inc=1, device_id=partner, device_id_type=MESH)
    plane_devices = [in_plane(step) for step in plane_steps]
    for device in plane_devices:
        pl.semaphore_signal(barrier, inc=1, device_id=device, device_id_type=MESH)
    for step in ring_steps:
        pl.semaphore_signal(barrier, inc=1, device_id=along_planes(step), device_id_type=MESH)

    for i, load in enumerate(e_loads):
        load.wait()
        part = pl.ds(i * 384, 384)
        ewide[part, :] = e_ref[part, :].astype(F32)
    sign_dn = jnp.where(t == 0, -1.0, 1.0).astype(F32)
    sign_up = jnp.where(t == nt - 1, -1.0, 1.0).astype(F32)

    def t_copy(way, z):
        return pltpu.make_async_remote_copy(
            src_ref=st.at[way, z],
            dst_ref=ht.at[way, z],
            send_sem=ts_sem.at[way, z],
            recv_sem=tr_sem.at[way, z],
            device_id=partners[way],
            device_id_type=MESH,
        )

    def z_copy(way):
        return pltpu.make_async_remote_copy(
            src_ref=sz.at[way],
            dst_ref=hz.at[way],
            send_sem=zs_sem.at[way],
            recv_sem=zr_sem.at[way],
            device_id=partners[2 + way],
            device_id_type=MESH,
        )

    def prepare(z):
        halves = []
        for g in range(2):
            halves.append(
                load_spin(
                    lambda comp: ewide[pl.ds((g * 8 * 24 + comp) * 4 + z, 8, stride=96), :]
                )
            )
        both = [
            [
                tuple(
                    jnp.concatenate([halves[0][a][c][q], halves[1][a][c][q]], axis=0)
                    for q in range(2)
                )
                for c in range(3)
            ]
            for a in range(4)
        ]
        for way, sign, factor in ((0, -1, sign_dn), (1, 1, sign_up)):
            half = project(both, 3, sign)
            for a in range(2):
                for c in range(3):
                    for q in range(2):
                        st[way, z, q * 6 + a * 3 + c] = (half[a][c][q] * factor).astype(BF16)
        for edge, way, sign in ((0, 0, -1), (ZL - 1, 1, 1)):
            if z == edge:
                half = project(both, 2, sign)
                for a in range(2):
                    for c in range(3):
                        for q in range(2):
                            sz[way, q * 6 + a * 3 + c] = half[a][c][q].astype(BF16)
        for a in range(4):
            for c in range(3):
                for q in range(2):
                    ef[z, q * 12 + a * 3 + c] = both[a][c][q]
                    e2[z, q * 12 + a * 3 + c] = both[a][c][q].astype(BF16)

    for z in (0, 3, 2, 1):
        prepare(z)
        if z == 0:
            pl.semaphore_wait(barrier, 2 + 31 + 7)
            z_copy(0).start()
        if z == ZL - 1:
            z_copy(1).start()
        for way in range(2):
            t_copy(way, z).start()

    loads[0].wait()
    phase_tables(t, s, momenta_ref[...], cos_ref, sin_ref)
    total_ref[...] = jnp.zeros_like(total_ref)

    def even_step(z, carry):
        meson_part(e2, 0, z, cos_ref, sin_ref, total_ref)
        return carry

    lax.fori_loop(0, ZL, even_step, 0)
    loads[1].wait()

    def widen_links(i, carry):
        rows = pl.ds(pl.multiple_of(i * 96, 96), 96)
        lf[rows, :] = links_ref[rows, :].astype(F32)
        return carry

    lax.fori_loop(0, 6, widen_links, 0)

    def z_halves(i, carry):
        z, g = i // 2, lax.rem(i, 2)
        rows = pl.ds(pl.multiple_of(g * 8, 8), 8)
        for way, sign, source, target in ((0, -1, z + 1, z), (1, 1, z, z + 1)):
            half = project(load_spin(lambda comp: ef[source, comp, rows, :]), 2, sign)
            for a in range(2):
                for c in range(3):
                    for q in range(2):
                        zf[way, target, q * 6 + a * 3 + c, rows, :] = half[a][c][q]
        return carry

    lax.fori_loop(0, 2 * (ZL - 1), z_halves, 0)
    for way in range(2):
        z_copy(way).wait_recv()
    zf[0, ZL - 1] = hz[0].astype(F32)
    zf[1, 0] = hz[1].astype(F32)
    lane = lax.broadcasted_iota(jnp.int32, (8, 128), 1)
    first, last = (lane & 7) == 0, (lane & 7) == 7

    def link(way, d, z):
        def load(q, a, b):
            row = ((((way * 4 + d) * 2 + q) * 3 + a) * 3 + b) * ZL
            return lf[pl.ds(row + z, 1), :]

        return load

    def stored(read):
        return [[(read(a * 3 + c), read(6 + a * 3 + c)) for c in range(3)] for a in range(2)]

    def near_step(i, carry):
        z, g = i // 2, lax.rem(i, 2)
        rows = pl.ds(pl.multiple_of(g * 8, 8), 8)
        shifted = ((t + s * ZL + z + (lane >> 3) + 1) & 1) == 1
        spin = load_spin(lambda comp: ef[z, comp, rows, :])
        zero = jnp.zeros((8, 128), F32)
        total = [[(zero, zero) for _ in range(3)] for _ in range(4)]

        def x_ahead(v):
            ahead = jnp.where(last, pltpu.roll(v, 7, 1), pltpu.roll(v, 127, 1))
            return jnp.where(shifted, ahead, v)

        def x_behind(v):
            behind = jnp.where(first, pltpu.roll(v, 121, 1), pltpu.roll(v, 1, 1))
            return jnp.where(shifted, v, behind)

        for way, sign in ((0, -1), (1, 1)):
            for d in range(3):
                if d == 0:
                    half = map_half(project(spin, 0, sign), (x_ahead, x_behind)[way])
                elif d == 1:
                    half = map_half(
                        project(spin, 1, sign), lambda v: pltpu.roll(v, (120, 8)[way], 1)
                    )
                else:
                    half = stored(lambda comp: zf[way, z, comp, rows, :])
                total = add_hop(total, link_times(link(way, d, z), half, way == 1), d, sign)
        for a in range(4):
            for c in range(3):
                for q in range(2):
                    of[z, q * 12 + a * 3 + c, rows, :] = total[a][c][q]
        return carry

    lax.fori_loop(0, 2 * ZL, near_step, 0)
    loads[2].wait()

    def far_step(i, carry):
        z = lax.rem(3 * i, ZL)
        for way in range(2):
            t_copy(way, z).wait_recv()
            tf[way] = ht[way, z].astype(F32)

        def group_step(g, carry):
            rows = pl.ds(pl.multiple_of(g * 8, 8), 8)
            total = load_spin(lambda comp: of[z, comp, rows, :])
            for way, sign in ((0, -1), (1, 1)):
                half = stored(lambda comp: tf[way, comp, rows, :])
                total = add_hop(total, link_times(link(way, 3, z), half, way == 1), 3, sign)
            for chir in range(2):
                source = [
                    tuple(hop_kappa * total[2 * chir + col // 3][col % 3][q] for q in range(2))
                    for col in range(6)
                ]
                for r in range(6):
                    out_real = out_imag = None
                    for col in range(6):
                        row = ((chir * 2 * 6 + r) * 6 + col) * ZL
                        cr = clover_ref[pl.ds(row + z, 1), :]
                        ci = clover_ref[pl.ds(row + 36 * ZL + z, 1), :]
                        vr, vi = source[col]
                        re, im = cr * vr - ci * vi, cr * vi + ci * vr
                        out_real = re if out_real is None else out_real + re
                        out_imag = im if out_imag is None else out_imag + im
                    place = 6 * chir + r
                    of[z, place, rows, :] = out_real
                    of[z, 12 + place, rows, :] = out_imag
            return carry

        lax.fori_loop(0, 2, group_step, 0)
        ob[z] = of[z].astype(BF16)
        meson_part(ob, 1, z, cos_ref, sin_ref, total_ref)
        return carry

    lax.fori_loop(0, ZL, far_step, 0)

    def send(stage, source, target, slot, device):
        pltpu.make_async_remote_copy(
            src_ref=source,
            dst_ref=target.at[slot],
            send_sem=x_send.at[stage],
            recv_sem=x_recv.at[stage],
            device_id=device,
            device_id_type=MESH,
        ).start()

    def wait(stage, target, count, sems):
        others = target.at[pl.ds(0, count)]
        pltpu.make_async_copy(others, others, sems.at[stage]).wait()

    def rows_of(index):
        return pl.ds(pl.multiple_of(index * 8, 8), 8)

    for device in plane_devices:
        send(0, total_ref.at[rows_of(lax.rem(device[0], 8) * 4 + device[1])], arr1, place, device)
    arr1[place] = total_ref[rows_of(place), :]

    def turn(comp, carry):
        for z in range(ZL):
            for g in range(2):
                lf[pl.ds(g * 32 + z, 8, stride=4), :] = of[z, comp, pl.ds(g * 8, 8), :]
        odd_ref[:, comp] = lf[pl.ds(0, 64), :].astype(BF16).reshape(NMODE, ZL, 128)
        return carry

    lax.fori_loop(0, 24, turn, 0)
    loads[3].wait()
    loads[4].wait()
    weights = weights_ref[...]
    lane16 = lax.broadcasted_iota(jnp.int32, (NMODE, 128), 1)
    spread = (lane16 % NMODE == lax.broadcasted_iota(jnp.int32, (NMODE, 128), 0)).astype(F32)
    weight_j = jnp.dot(weights, spread, precision=lax.Precision.HIGHEST, preferred_element_type=F32)
    mode = lax.broadcasted_iota(jnp.int32, (1, NMODE), 1)
    pair_weights = [
        jnp.sum(
            jnp.where(mode == lax.rem(place, 2) * 8 + r, weights, 0.0), axis=1, keepdims=True
        )
        * weight_j
        for r in range(8)
    ]
    across = lax.broadcasted_iota(jnp.int32, (16, 16), 1)
    diagonal = across == lax.broadcasted_iota(jnp.int32, (16, 16), 0)
    separation = jnp.sum(
        jnp.where(diagonal, sep_ref[...].astype(F32), 0.0), axis=1, keepdims=True
    ).astype(jnp.int32)
    chosen = lax.broadcasted_iota(jnp.int32, (16, 128), 1) == lax.rem(t + separation, nt)
    for way in range(2):
        z_copy(way).wait_send()
        for z in range(ZL):
            t_copy(way, z).wait_send()
    wait(0, arr1, 31, x_recv)
    for j in range(8):
        field = arr1[4 * j] + arr1[4 * j + 1] + arr1[4 * j + 2] + arr1[4 * j + 3]
        turn2[pl.ds(j, 8, stride=8), :] = field
    send2[...] = turn2[...].astype(BF16)
    for step in ring_steps:
        send(1, send2, arr2, tz, along_planes(step))
    arr2[tz] = send2[...]
    own = send2[...].astype(F32)
    weighted = [own[8 * r : 8 * r + 8] * pair_weights[r] for r in range(8)]
    high = [v.astype(BF16) for v in weighted]
    low = [(v - h.astype(F32)).astype(BF16) for v, h in zip(weighted, high)]
    sources = jnp.concatenate(
        [jnp.concatenate(high, axis=1), jnp.concatenate(low, axis=1)], axis=0
    )
    gathered[...] = jnp.zeros_like(gathered)
    wait(0, arr1, 31, x_send)
    wait(1, arr2, 7, x_recv)
    planes = [arr2[i].astype(F32) for i in range(8)]
    sinks = jnp.concatenate(
        [
            jnp.concatenate([planes[i][8 * r : 8 * r + 8] for i in range(8)], axis=0).astype(BF16)
            for r in range(8)
        ],
        axis=1,
    )
    product = lax.dot_general(
        sources, sinks, (((1,), (1,)), ((), ())), preferred_element_type=F32
    )
    gathered[:, :64] = product[:8] + product[8:]
    for j in range(8):
        send3[j] = gathered[pl.ds(j, 1), :]
    for device in plane_devices:
        send(2, send3.at[lax.rem(device[0], 8)], arr3, place, device)
    arr3[place] = send3[lax.rem(t, 8)]
    wait(1, arr2, 7, x_send)
    wait(2, arr3, 31, x_recv)
    row = jnp.sum(arr3[...], axis=0)
    picked = jnp.sum(jnp.where(chosen, row, 0.0), axis=1, keepdims=True)
    out_ref[...] = jnp.sum(jnp.where(diagonal, picked, 0.0), axis=0, keepdims=True) * (
        1.0 / (16.0 * NMODE * NMOM * LS**3)
    )
    wait(2, arr3, 31, x_send)


def finish_kernel(odd_ref, row_ref, odd_out, row_out, sems):
    copies = [
        pltpu.make_async_copy(odd_ref, odd_out, sems.at[0]),
        pltpu.make_async_copy(row_ref, row_out, sems.at[1]),
    ]
    for copy in copies:
        copy.start()
    for copy in copies:
        copy.wait()


def body(nt, ns, even_modes, hop_links, clover_inverse, momenta, mode_weights, separations):
    vmem = pl.BlockSpec(memory_space=pltpu.VMEM)
    hbm = pl.BlockSpec(memory_space=pltpu.HBM)
    shape = jax.ShapeDtypeStruct
    dma = pltpu.SemaphoreType.DMA
    sites = (ZL, 24, NMODE, 128)
    odd_modes, correlator = pl.pallas_call(
        functools.partial(kernel, nt, ns),
        out_shape=(pltpu.VMEM((NMODE, 24, ZL, 128), BF16), pltpu.VMEM((1, 16), F32)),
        in_specs=[hbm] * 6,
        out_specs=(vmem, vmem),
        scratch_shapes=[
            pltpu.VMEM((NMODE * 24 * ZL, 128), BF16),
            pltpu.VMEM((144 * ZL, 128), BF16),
            pltpu.VMEM((144 * ZL, 128), F32),
            pltpu.VMEM((3, NMOM), jnp.int32),
            pltpu.VMEM((1, NMODE), F32),
            pltpu.VMEM((1, 16), jnp.int32),
            pltpu.VMEM(sites, F32),
            pltpu.VMEM((NMODE * 24 * ZL, 128), F32),
            pltpu.VMEM(sites, BF16),
            pltpu.VMEM((2, ZL, 12, NMODE, 128), BF16),
            pltpu.VMEM((2, 12, NMODE, 128), BF16),
            pltpu.VMEM((2, ZL, 12, NMODE, 128), BF16),
            pltpu.VMEM((2, 12, NMODE, 128), BF16),
            pltpu.VMEM((2, 12, NMODE, 128), F32),
            pltpu.VMEM((2, ZL, 12, NMODE, 128), F32),
            pltpu.VMEM((144 * ZL, 128), F32),
            pltpu.VMEM(sites, F32),
            pltpu.VMEM(sites, BF16),
            pltpu.VMEM((2, ZL, NMOM, 128), F32),
            pltpu.VMEM((2, ZL, NMOM, 128), F32),
            pltpu.VMEM((NMOM * NMODE, 128), F32),
            pltpu.VMEM((32, 8, 128), F32),
            pltpu.VMEM((64, 128), F32),
            pltpu.VMEM((64, 128), BF16),
            pltpu.VMEM((8, 64, 128), BF16),
            pltpu.VMEM((8, 128), F32),
            pltpu.VMEM((8, 1, 128), F32),
            pltpu.VMEM((32, 1, 128), F32),
            dma((4,)), dma((5,)), dma((2, ZL)), dma((2, ZL)), dma((2,)), dma((2,)), dma((3,)), dma((3,)),
        ],
        compiler_params=pltpu.CompilerParams(
            collective_id=0, has_side_effects=True, vmem_limit_bytes=63 * 1024 * 1024
        ),
        name="correlator",
    )(
        even_modes.reshape(NMODE * 24 * ZL, 128),
        hop_links.reshape(144 * ZL, 128),
        clover_inverse.reshape(144 * ZL, 128),
        momenta.T,
        mode_weights.reshape(1, NMODE),
        separations,
    )
    odd_modes, correlator = pl.pallas_call(
        finish_kernel,
        out_shape=(shape(odd_modes.shape, BF16), shape((1, 16), F32)),
        in_specs=[vmem, vmem],
        out_specs=(hbm, hbm),
        scratch_shapes=[dma((2,))],
        compiler_params=pltpu.CompilerParams(vmem_limit_bytes=1024 * 1024),
        name="finish",
    )(odd_modes, correlator)
    return odd_modes.reshape(even_modes.shape), correlator


def solution(mesh):
    in_specs = (
        P(None, None, None, None, "ta", "sa", None),
        P(None, None, None, None, None, "ta", "sa", None),
        P(None, None, None, None, "ta", "sa", None),
        P(),
        P(),
        P("ta", None),
    )
    out_specs = (P(None, None, None, None, "ta", "sa", None), P("ta", None))
    return jax.shard_map(
        functools.partial(body, mesh.shape["ta"], mesh.shape["sa"]),
        mesh=mesh,
        in_specs=in_specs,
        out_specs=out_specs,
        check_vma=False,
    )
```

```python
import functools
import math

import jax
import jax.numpy as jnp
from jax import lax
from jax.experimental import pallas as pl
from jax.experimental.pallas import tpu as pltpu
from jax.sharding import PartitionSpec as P

NMODE = 16
NMOM = 16
LS = 16
ZL = 4
F32 = jnp.float32
BF16 = jnp.bfloat16
MESH = pl.DeviceIdType.MESH

hop_kappa = 0.125
gamma_source = ((3, 2, 1, 0), (3, 2, 1, 0), (2, 3, 0, 1), (2, 3, 0, 1))
gamma_factor = ((3, 3, 2, 2), (1, 0, 0, 1), (3, 2, 2, 3), (0, 0, 0, 0))
factor_parts = ((1, 0), (-1, 0), (0, 1), (0, -1))


def add_factor(base, value, code, sign):
    (br, bi), (vr, vi) = base, value
    re, im = factor_parts[code]
    re, im = re * sign, im * sign
    if re == 1:
        return br + vr, bi + vi
    if re == -1:
        return br - vr, bi - vi
    if im == 1:
        return br - vi, bi + vr
    return br + vi, bi - vr


def project(spin, d, sign):
    return [
        [
            add_factor(spin[s][c], spin[gamma_source[d][s]][c], gamma_factor[d][s], sign)
            for c in range(3)
        ]
        for s in range(2)
    ]


def load_spin(load):
    return [[(load(s * 3 + c), load(12 + s * 3 + c)) for c in range(3)] for s in range(4)]


def link_times(load, half, adjoint):
    out = [[None] * 3 for _ in range(2)]
    for a in range(3):
        for b in range(3):
            lr, li = (load(0, b, a), load(1, b, a)) if adjoint else (load(0, a, b), load(1, a, b))
            for s in range(2):
                hr, hi = half[s][b]
                if adjoint:
                    re, im = lr * hr + li * hi, lr * hi - li * hr
                else:
                    re, im = lr * hr - li * hi, lr * hi + li * hr
                old = out[s][a]
                out[s][a] = (re, im) if old is None else (old[0] + re, old[1] + im)
    return out


def add_hop(total, half, d, sign):
    for s in range(2):
        for c in range(3):
            total[s][c] = (total[s][c][0] + half[s][c][0], total[s][c][1] + half[s][c][1])
    for s in range(2, 4):
        for c in range(3):
            total[s][c] = add_factor(
                total[s][c], half[gamma_source[d][s]][c], gamma_factor[d][s], sign
            )
    return total


def map_half(half, f):
    return [[(f(half[s][c][0]), f(half[s][c][1])) for c in range(3)] for s in range(2)]


def circle(step):
    fold = jnp.where(step > 8, 16 - step, step)
    low = jnp.where(fold > 4, 8 - fold, fold)
    value = jnp.where(low == 1, math.cos(math.pi / 8), 1.0).astype(F32)
    value = jnp.where(low == 2, math.cos(math.pi / 4), value).astype(F32)
    value = jnp.where(low == 3, math.cos(3 * math.pi / 8), value).astype(F32)
    value = jnp.where(low == 4, 0.0, value).astype(F32)
    return jnp.where(fold > 4, -value, value)


def phase_tables(t, s, momenta, cos_ref, sin_ref):
    lane = lax.broadcasted_iota(jnp.int32, (NMOM, 128), 1)
    y, h = lane >> 3, lane & 7
    place = lax.broadcasted_iota(jnp.int32, (NMOM, NMOM), 1)
    diagonal = place == lax.broadcasted_iota(jnp.int32, (NMOM, NMOM), 0)
    nx, ny, nz = (
        jnp.sum(
            jnp.where(diagonal, momenta[d : d + 1, :].astype(F32), 0.0), axis=1, keepdims=True
        ).astype(jnp.int32)
        for d in range(3)
    )
    for parity in range(2):
        for zl in range(ZL):
            z = s * ZL + zl
            x = 2 * h + ((t + z + y + parity) & 1)
            step = (nx * x + ny * y + nz * z) & 15
            cos_ref[parity, zl] = circle(step)
            sin_ref[parity, zl] = circle((step + 12) & 15)


def meson_part(modes_ref, parity, z, cos_ref, sin_ref, total_ref):
    for a in range(4):
        for c in range(3):
            comp = a * 3 + c
            vr = modes_ref[z, comp].astype(F32)
            vi = modes_ref[z, 12 + comp].astype(F32)
            rows = []
            for p in range(NMOM):
                cs = cos_ref[parity, z, pl.ds(p, 1), :]
                sn = sin_ref[parity, z, pl.ds(p, 1), :]
                rows.append(
                    jnp.concatenate(
                        [
                            (vr * cs - vi * sn).astype(BF16),
                            (-(vr * sn + vi * cs)).astype(BF16),
                        ],
                        axis=1,
                    )
                )
            left = jnp.concatenate(rows, axis=0)
            real_rows, imag_rows = [], []
            for k in range(4):
                other = gamma_source[k][a] * 3 + c
                wr = modes_ref[z, other]
                wi = modes_ref[z, 12 + other]
                re, im = factor_parts[gamma_factor[k][a]]
                if re == 1:
                    gr, gi = wr, wi
                elif re == -1:
                    gr, gi = -wr, -wi
                elif im == 1:
                    gr, gi = -wi, wr
                else:
                    gr, gi = wi, -wr
                real_rows.append(jnp.concatenate([gr, -gi], axis=1))
                imag_rows.append(jnp.concatenate([gi, gr], axis=1))
            right = jnp.concatenate(real_rows + imag_rows, axis=0)
            total_ref[...] += lax.dot_general(
                left, right, (((1,), (1,)), ((), ())), preferred_element_type=F32
            )


def plane_distance(step):
    dy, dx, dn, dc = step
    return -(min(dy, 4 - dy) + (2 * dx if not dn else 1)), -dc


plane_steps = sorted(
    [
        (dy, dx, dn, dc)
        for dy in range(4)
        for dx in range(2)
        for dn in range(2)
        for dc in range(2)
        if dy or dx or dn or dc
    ],
    key=plane_distance,
)
ring_steps = (4, 3, 5, 2, 6, 1, 7)


def kernel(
    nt, ns,
    e_hbm, links_hbm, clover_hbm, momenta_hbm, weights_hbm, sep_hbm,
    odd_ref, out_ref,
    e_ref, links_ref, clover_ref, momenta_ref, weights_ref, sep_ref,
    ef, ewide, e2, st, sz, ht, hz, tf, zf, lf, of, ob, cos_ref, sin_ref,
    total_ref, arr1, turn2, send2, arr2, gathered, send3, arr3,
    e_sem, in_sem, ts_sem, tr_sem, zs_sem, zr_sem, x_send, x_recv,
):
    t = lax.axis_index("ta")
    s = lax.axis_index("sa")
    tz, ty, tx = t // 8, lax.rem(t, 8) // 2, lax.rem(t, 2)
    t_up, t_dn = lax.rem(t + 1, nt), lax.rem(t + nt - 1, nt)
    s_up, s_dn = lax.rem(s + 1, ns), lax.rem(s + ns - 1, ns)
    partners = ((t_dn, s), (t_up, s), (t, s_dn), (t, s_up))
    place = lax.rem(t, 8) * 4 + s

    def in_plane(step):
        dy, dx, dn, dc = step
        x_half, x_near, core = lax.rem(tx + dx, 2), lax.rem(s // 2 + dn, 2), lax.rem(s + dc, 2)
        return tz * 8 + lax.rem(ty + dy, 4) * 2 + x_half, x_near * 2 + core

    def along_planes(step):
        return lax.rem(tz + step, 8) * 8 + lax.rem(t, 8), s

    loads = []
    e_loads = []
    for i in range(4):
        part = pl.ds(i * 384, 384)
        load = pltpu.make_async_copy(e_hbm.at[part], e_ref.at[part], e_sem.at[i])
        load.start()
        e_loads.append(load)
    for i, (source, target) in enumerate(
        (
            (momenta_hbm, momenta_ref), (links_hbm, links_ref), (clover_hbm, clover_ref),
            (weights_hbm, weights_ref), (sep_hbm, sep_ref),
        )
    ):
        load = pltpu.make_async_copy(source, target, in_sem.at[i])
        load.start()
        loads.append(load)
    barrier = pltpu.get_barrier_semaphore()
    for partner in partners[:2]:
        pl.semaphore_signal(barrier, inc=1, device_id=partner, device_id_type=MESH)
    plane_devices = [in_plane(step) for step in plane_steps]
    for device in plane_devices:
        pl.semaphore_signal(barrier, inc=1, device_id=device, device_id_type=MESH)
    for step in ring_steps:
        pl.semaphore_signal(barrier, inc=1, device_id=along_planes(step), device_id_type=MESH)

    for i, load in enumerate(e_loads):
        load.wait()
        part = pl.ds(i * 384, 384)
        ewide[part, :] = e_ref[part, :].astype(F32)
    sign_dn = jnp.where(t == 0, -1.0, 1.0).astype(F32)
    sign_up = jnp.where(t == nt - 1, -1.0, 1.0).astype(F32)

    def t_copy(way, z):
        return pltpu.make_async_remote_copy(
            src_ref=st.at[way, z],
            dst_ref=ht.at[way, z],
            send_sem=ts_sem.at[way, z],
            recv_sem=tr_sem.at[way, z],
            device_id=partners[way],
            device_id_type=MESH,
        )

    def z_copy(way):
        return pltpu.make_async_remote_copy(
            src_ref=sz.at[way],
            dst_ref=hz.at[way],
            send_sem=zs_sem.at[way],
            recv_sem=zr_sem.at[way],
            device_id=partners[2 + way],
            device_id_type=MESH,
        )

    def prepare(z):
        halves = []
        for g in range(2):
            halves.append(
                load_spin(
                    lambda comp: ewide[pl.ds((g * 8 * 24 + comp) * 4 + z, 8, stride=96), :]
                )
            )
        both = [
            [
                tuple(
                    jnp.concatenate([halves[0][a][c][q], halves[1][a][c][q]], axis=0)
                    for q in range(2)
                )
                for c in range(3)
            ]
            for a in range(4)
        ]
        for way, sign, factor in ((0, -1, sign_dn), (1, 1, sign_up)):
            half = project(both, 3, sign)
            for a in range(2):
                for c in range(3):
                    for q in range(2):
                        st[way, z, q * 6 + a * 3 + c] = (half[a][c][q] * factor).astype(BF16)
        for edge, way, sign in ((0, 0, -1), (ZL - 1, 1, 1)):
            if z == edge:
                half = project(both, 2, sign)
                for a in range(2):
                    for c in range(3):
                        for q in range(2):
                            sz[way, q * 6 + a * 3 + c] = half[a][c][q].astype(BF16)
        for a in range(4):
            for c in range(3):
                for q in range(2):
                    ef[z, q * 12 + a * 3 + c] = both[a][c][q]
                    e2[z, q * 12 + a * 3 + c] = both[a][c][q].astype(BF16)

    for z in (0, 3, 2, 1):
        prepare(z)
        if z == 0:
            pl.semaphore_wait(barrier, 2 + 31 + 7)
            z_copy(0).start()
        if z == ZL - 1:
            z_copy(1).start()
        for way in range(2):
            t_copy(way, z).start()

    loads[0].wait()
    phase_tables(t, s, momenta_ref[...], cos_ref, sin_ref)
    total_ref[...] = jnp.zeros_like(total_ref)

    def even_step(z, carry):
        meson_part(e2, 0, z, cos_ref, sin_ref, total_ref)
        return carry

    lax.fori_loop(0, ZL, even_step, 0)
    loads[1].wait()

    def widen_links(i, carry):
        rows = pl.ds(pl.multiple_of(i * 96, 96), 96)
        lf[rows, :] = links_ref[rows, :].astype(F32)
        return carry

    lax.fori_loop(0, 6, widen_links, 0)

    def z_halves(i, carry):
        z, g = i // 2, lax.rem(i, 2)
        rows = pl.ds(pl.multiple_of(g * 8, 8), 8)
        for way, sign, source, target in ((0, -1, z + 1, z), (1, 1, z, z + 1)):
            half = project(load_spin(lambda comp: ef[source, comp, rows, :]), 2, sign)
            for a in range(2):
                for c in range(3):
                    for q in range(2):
                        zf[way, target, q * 6 + a * 3 + c, rows, :] = half[a][c][q]
        return carry

    lax.fori_loop(0, 2 * (ZL - 1), z_halves, 0)
    for way in range(2):
        z_copy(way).wait_recv()
    zf[0, ZL - 1] = hz[0].astype(F32)
    zf[1, 0] = hz[1].astype(F32)
    lane = lax.broadcasted_iota(jnp.int32, (8, 128), 1)
    first, last = (lane & 7) == 0, (lane & 7) == 7

    def link(way, d, z):
        def load(q, a, b):
            row = ((((way * 4 + d) * 2 + q) * 3 + a) * 3 + b) * ZL
            return lf[pl.ds(row + z, 1), :]

        return load

    def stored(read):
        return [[(read(a * 3 + c), read(6 + a * 3 + c)) for c in range(3)] for a in range(2)]

    def near_step(i, carry):
        z, g = i // 2, lax.rem(i, 2)
        rows = pl.ds(pl.multiple_of(g * 8, 8), 8)
        shifted = ((t + s * ZL + z + (lane >> 3) + 1) & 1) == 1
        spin = load_spin(lambda comp: ef[z, comp, rows, :])
        zero = jnp.zeros((8, 128), F32)
        total = [[(zero, zero) for _ in range(3)] for _ in range(4)]

        def x_ahead(v):
            ahead = jnp.where(last, pltpu.roll(v, 7, 1), pltpu.roll(v, 127, 1))
            return jnp.where(shifted, ahead, v)

        def x_behind(v):
            behind = jnp.where(first, pltpu.roll(v, 121, 1), pltpu.roll(v, 1, 1))
            return jnp.where(shifted, v, behind)

        for way, sign in ((0, -1), (1, 1)):
            for d in range(3):
                if d == 0:
                    half = map_half(project(spin, 0, sign), (x_ahead, x_behind)[way])
                elif d == 1:
                    half = map_half(
                        project(spin, 1, sign), lambda v: pltpu.roll(v, (120, 8)[way], 1)
                    )
                else:
                    half = stored(lambda comp: zf[way, z, comp, rows, :])
                total = add_hop(total, link_times(link(way, d, z), half, way == 1), d, sign)
        for a in range(4):
            for c in range(3):
                for q in range(2):
                    of[z, q * 12 + a * 3 + c, rows, :] = total[a][c][q]
        return carry

    lax.fori_loop(0, 2 * ZL, near_step, 0)
    loads[2].wait()

    def far_step(i, carry):
        z = lax.rem(3 * i, ZL)
        for way in range(2):
            t_copy(way, z).wait_recv()
            tf[way] = ht[way, z].astype(F32)

        def group_step(g, carry):
            rows = pl.ds(pl.multiple_of(g * 8, 8), 8)
            total = load_spin(lambda comp: of[z, comp, rows, :])
            for way, sign in ((0, -1), (1, 1)):
                half = stored(lambda comp: tf[way, comp, rows, :])
                total = add_hop(total, link_times(link(way, 3, z), half, way == 1), 3, sign)
            for chir in range(2):
                source = [
                    tuple(hop_kappa * total[2 * chir + col // 3][col % 3][q] for q in range(2))
                    for col in range(6)
                ]
                for r in range(6):
                    out_real = out_imag = None
                    for col in range(6):
                        row = ((chir * 2 * 6 + r) * 6 + col) * ZL
                        cr = clover_ref[pl.ds(row + z, 1), :]
                        ci = clover_ref[pl.ds(row + 36 * ZL + z, 1), :]
                        vr, vi = source[col]
                        re, im = cr * vr - ci * vi, cr * vi + ci * vr
                        out_real = re if out_real is None else out_real + re
                        out_imag = im if out_imag is None else out_imag + im
                    place = 6 * chir + r
                    of[z, place, rows, :] = out_real
                    of[z, 12 + place, rows, :] = out_imag
            return carry

        lax.fori_loop(0, 2, group_step, 0)
        ob[z] = of[z].astype(BF16)
        meson_part(ob, 1, z, cos_ref, sin_ref, total_ref)
        return carry

    lax.fori_loop(0, ZL, far_step, 0)

    def send(stage, source, target, slot, device):
        pltpu.make_async_remote_copy(
            src_ref=source,
            dst_ref=target.at[slot],
            send_sem=x_send.at[stage],
            recv_sem=x_recv.at[stage],
            device_id=device,
            device_id_type=MESH,
        ).start()

    def wait(stage, target, count, sems):
        others = target.at[pl.ds(0, count)]
        pltpu.make_async_copy(others, others, sems.at[stage]).wait()

    def rows_of(index):
        return pl.ds(pl.multiple_of(index * 8, 8), 8)

    for device in plane_devices:
        send(0, total_ref.at[rows_of(lax.rem(device[0], 8) * 4 + device[1])], arr1, place, device)
    arr1[place] = total_ref[rows_of(place), :]

    def turn(comp, carry):
        for z in range(ZL):
            for g in range(2):
                lf[pl.ds(g * 32 + z, 8, stride=4), :] = of[z, comp, pl.ds(g * 8, 8), :]
        odd_ref[:, comp] = lf[pl.ds(0, 64), :].astype(BF16).reshape(NMODE, ZL, 128)
        return carry

    lax.fori_loop(0, 24, turn, 0)
    loads[3].wait()
    loads[4].wait()
    weights = weights_ref[...]
    lane16 = lax.broadcasted_iota(jnp.int32, (NMODE, 128), 1)
    spread = (lane16 % NMODE == lax.broadcasted_iota(jnp.int32, (NMODE, 128), 0)).astype(F32)
    weight_j = jnp.dot(weights, spread, precision=lax.Precision.HIGHEST, preferred_element_type=F32)
    mode = lax.broadcasted_iota(jnp.int32, (1, NMODE), 1)
    pair_weights = [
        jnp.sum(
            jnp.where(mode == lax.rem(place, 2) * 8 + r, weights, 0.0), axis=1, keepdims=True
        )
        * weight_j
        for r in range(8)
    ]
    across = lax.broadcasted_iota(jnp.int32, (16, 16), 1)
    diagonal = across == lax.broadcasted_iota(jnp.int32, (16, 16), 0)
    separation = jnp.sum(
        jnp.where(diagonal, sep_ref[...].astype(F32), 0.0), axis=1, keepdims=True
    ).astype(jnp.int32)
    chosen = lax.broadcasted_iota(jnp.int32, (16, 128), 1) == lax.rem(t + separation, nt)
    for way in range(2):
        z_copy(way).wait_send()
        for z in range(ZL):
            t_copy(way, z).wait_send()
    wait(0, arr1, 31, x_recv)
    for j in range(8):
        field = arr1[4 * j] + arr1[4 * j + 1] + arr1[4 * j + 2] + arr1[4 * j + 3]
        turn2[pl.ds(j, 8, stride=8), :] = field
    send2[...] = turn2[pl.ds(0, 64), :].astype(BF16)
    for step in ring_steps:
        send(1, send2, arr2, tz, along_planes(step))
    arr2[tz] = send2[...]
    own = send2[...].astype(F32)
    weighted = [own[8 * r : 8 * r + 8] * pair_weights[r] for r in range(8)]
    high = [v.astype(BF16) for v in weighted]
    low = [(v - h.astype(F32)).astype(BF16) for v, h in zip(weighted, high)]
    sources = jnp.concatenate(
        [jnp.concatenate(high, axis=1), jnp.concatenate(low, axis=1)], axis=0
    )
    gathered[...] = jnp.zeros_like(gathered)
    wait(0, arr1, 31, x_send)
    wait(1, arr2, 7, x_recv)
    planes = [arr2[i].astype(F32) for i in range(8)]
    sinks = jnp.concatenate(
        [
            jnp.concatenate([planes[i][8 * r : 8 * r + 8] for i in range(8)], axis=0).astype(BF16)
            for r in range(8)
        ],
        axis=1,
    )
    product = lax.dot_general(
        sources, sinks, (((1,), (1,)), ((), ())), preferred_element_type=F32
    )
    gathered[:, :64] = product[:8] + product[8:]
    for j in range(8):
        send3[j] = gathered[pl.ds(j, 1), :]
    for device in plane_devices:
        send(2, send3.at[lax.rem(device[0], 8)], arr3, place, device)
    arr3[place] = send3[lax.rem(t, 8)]
    wait(1, arr2, 7, x_send)
    wait(2, arr3, 31, x_recv)
    row = jnp.sum(arr3[...], axis=0)
    picked = jnp.sum(jnp.where(chosen, row, 0.0), axis=1, keepdims=True)
    out_ref[...] = jnp.sum(jnp.where(diagonal, picked, 0.0), axis=0, keepdims=True) * (
        1.0 / (16.0 * NMODE * NMOM * LS**3)
    )
    wait(2, arr3, 31, x_send)


def finish_kernel(odd_ref, row_ref, odd_out, row_out, sems):
    copies = [
        pltpu.make_async_copy(odd_ref, odd_out, sems.at[0]),
        pltpu.make_async_copy(row_ref, row_out, sems.at[1]),
    ]
    for copy in copies:
        copy.start()
    for copy in copies:
        copy.wait()


def body(nt, ns, even_modes, hop_links, clover_inverse, momenta, mode_weights, separations):
    vmem = pl.BlockSpec(memory_space=pltpu.VMEM)
    hbm = pl.BlockSpec(memory_space=pltpu.HBM)
    shape = jax.ShapeDtypeStruct
    dma = pltpu.SemaphoreType.DMA
    sites = (ZL, 24, NMODE, 128)
    odd_modes, correlator = pl.pallas_call(
        functools.partial(kernel, nt, ns),
        out_shape=(pltpu.VMEM((NMODE, 24, ZL, 128), BF16), pltpu.VMEM((1, 16), F32)),
        in_specs=[hbm] * 6,
        out_specs=(vmem, vmem),
        scratch_shapes=[
            pltpu.VMEM((NMODE * 24 * ZL, 128), BF16),
            pltpu.VMEM((144 * ZL, 128), BF16),
            pltpu.VMEM((144 * ZL, 128), F32),
            pltpu.VMEM((3, NMOM), jnp.int32),
            pltpu.VMEM((1, NMODE), F32),
            pltpu.VMEM((1, 16), jnp.int32),
            pltpu.VMEM(sites, F32),
            pltpu.VMEM(((NMODE + 1) * 24 * ZL, 128), F32),
            pltpu.VMEM(sites, BF16),
            pltpu.VMEM((2, ZL, 12, NMODE, 128), BF16),
            pltpu.VMEM((2, 12, NMODE, 128), BF16),
            pltpu.VMEM((2, ZL, 12, NMODE, 128), BF16),
            pltpu.VMEM((2, 12, NMODE, 128), BF16),
            pltpu.VMEM((2, 12, NMODE, 128), F32),
            pltpu.VMEM((2, ZL, 12, NMODE, 128), F32),
            pltpu.VMEM((144 * ZL, 128), F32),
            pltpu.VMEM(sites, F32),
            pltpu.VMEM(sites, BF16),
            pltpu.VMEM((2, ZL, NMOM, 128), F32),
            pltpu.VMEM((2, ZL, NMOM, 128), F32),
            pltpu.VMEM((NMOM * NMODE, 128), F32),
            pltpu.VMEM((32, 8, 128), F32),
            pltpu.VMEM((72, 128), F32),
            pltpu.VMEM((64, 128), BF16),
            pltpu.VMEM((8, 64, 128), BF16),
            pltpu.VMEM((8, 128), F32),
            pltpu.VMEM((8, 1, 128), F32),
            pltpu.VMEM((32, 1, 128), F32),
            dma((4,)), dma((5,)), dma((2, ZL)), dma((2, ZL)), dma((2,)), dma((2,)), dma((3,)), dma((3,)),
        ],
        compiler_params=pltpu.CompilerParams(
            collective_id=0, has_side_effects=True, vmem_limit_bytes=63 * 1024 * 1024
        ),
        name="correlator",
    )(
        even_modes.reshape(NMODE * 24 * ZL, 128),
        hop_links.reshape(144 * ZL, 128),
        clover_inverse.reshape(144 * ZL, 128),
        momenta.T,
        mode_weights.reshape(1, NMODE),
        separations,
    )
    odd_modes, correlator = pl.pallas_call(
        finish_kernel,
        out_shape=(shape(odd_modes.shape, BF16), shape((1, 16), F32)),
        in_specs=[vmem, vmem],
        out_specs=(hbm, hbm),
        scratch_shapes=[dma((2,))],
        compiler_params=pltpu.CompilerParams(vmem_limit_bytes=1024 * 1024),
        name="finish",
    )(odd_modes, correlator)
    return odd_modes.reshape(even_modes.shape), correlator


def solution(mesh):
    in_specs = (
        P(None, None, None, None, "ta", "sa", None),
        P(None, None, None, None, None, "ta", "sa", None),
        P(None, None, None, None, "ta", "sa", None),
        P(),
        P(),
        P("ta", None),
    )
    out_specs = (P(None, None, None, None, "ta", "sa", None), P("ta", None))
    return jax.shard_map(
        functools.partial(body, mesh.shape["ta"], mesh.shape["sa"]),
        mesh=mesh,
        in_specs=in_specs,
        out_specs=out_specs,
        check_vma=False,
    )
```

```python
import functools
import math

import jax
import jax.numpy as jnp
from jax import lax
from jax.experimental import pallas as pl
from jax.experimental.pallas import tpu as pltpu
from jax.sharding import PartitionSpec as P

NMODE = 16
NMOM = 16
LS = 16
ZL = 4
F32 = jnp.float32
BF16 = jnp.bfloat16
MESH = pl.DeviceIdType.MESH

hop_kappa = 0.125
gamma_source = ((3, 2, 1, 0), (3, 2, 1, 0), (2, 3, 0, 1), (2, 3, 0, 1))
gamma_factor = ((3, 3, 2, 2), (1, 0, 0, 1), (3, 2, 2, 3), (0, 0, 0, 0))
factor_parts = ((1, 0), (-1, 0), (0, 1), (0, -1))


def add_factor(base, value, code, sign):
    (br, bi), (vr, vi) = base, value
    re, im = factor_parts[code]
    re, im = re * sign, im * sign
    if re == 1:
        return br + vr, bi + vi
    if re == -1:
        return br - vr, bi - vi
    if im == 1:
        return br - vi, bi + vr
    return br + vi, bi - vr


def project(spin, d, sign):
    return [
        [
            add_factor(spin[s][c], spin[gamma_source[d][s]][c], gamma_factor[d][s], sign)
            for c in range(3)
        ]
        for s in range(2)
    ]


def load_spin(load):
    return [[(load(s * 3 + c), load(12 + s * 3 + c)) for c in range(3)] for s in range(4)]


def link_times(load, half, adjoint):
    out = [[None] * 3 for _ in range(2)]
    for a in range(3):
        for b in range(3):
            lr, li = (load(0, b, a), load(1, b, a)) if adjoint else (load(0, a, b), load(1, a, b))
            for s in range(2):
                hr, hi = half[s][b]
                if adjoint:
                    re, im = lr * hr + li * hi, lr * hi - li * hr
                else:
                    re, im = lr * hr - li * hi, lr * hi + li * hr
                old = out[s][a]
                out[s][a] = (re, im) if old is None else (old[0] + re, old[1] + im)
    return out


def add_hop(total, half, d, sign):
    for s in range(2):
        for c in range(3):
            total[s][c] = (total[s][c][0] + half[s][c][0], total[s][c][1] + half[s][c][1])
    for s in range(2, 4):
        for c in range(3):
            total[s][c] = add_factor(
                total[s][c], half[gamma_source[d][s]][c], gamma_factor[d][s], sign
            )
    return total


def map_half(half, f):
    return [[(f(half[s][c][0]), f(half[s][c][1])) for c in range(3)] for s in range(2)]


def circle(step):
    fold = jnp.where(step > 8, 16 - step, step)
    low = jnp.where(fold > 4, 8 - fold, fold)
    value = jnp.where(low == 1, math.cos(math.pi / 8), 1.0).astype(F32)
    value = jnp.where(low == 2, math.cos(math.pi / 4), value).astype(F32)
    value = jnp.where(low == 3, math.cos(3 * math.pi / 8), value).astype(F32)
    value = jnp.where(low == 4, 0.0, value).astype(F32)
    return jnp.where(fold > 4, -value, value)


def phase_tables(t, s, momenta, cos_ref, sin_ref):
    lane = lax.broadcasted_iota(jnp.int32, (NMOM, 128), 1)
    y, h = lane >> 3, lane & 7
    place = lax.broadcasted_iota(jnp.int32, (NMOM, NMOM), 1)
    diagonal = place == lax.broadcasted_iota(jnp.int32, (NMOM, NMOM), 0)
    nx, ny, nz = (
        jnp.sum(
            jnp.where(diagonal, momenta[d : d + 1, :].astype(F32), 0.0), axis=1, keepdims=True
        ).astype(jnp.int32)
        for d in range(3)
    )
    for parity in range(2):
        for zl in range(ZL):
            z = s * ZL + zl
            x = 2 * h + ((t + z + y + parity) & 1)
            step = (nx * x + ny * y + nz * z) & 15
            cos_ref[parity, zl] = circle(step)
            sin_ref[parity, zl] = circle((step + 12) & 15)


def meson_part(modes_ref, parity, z, cos_ref, sin_ref, total_ref, p0=0, count=NMOM):
    first = p0 * NMODE if isinstance(p0, int) else pl.multiple_of(p0 * NMODE, 128)
    for a in range(4):
        for c in range(3):
            comp = a * 3 + c
            vr = modes_ref[z, comp].astype(F32)
            vi = modes_ref[z, 12 + comp].astype(F32)
            rows = []
            for p in range(count):
                cs = cos_ref[parity, z, pl.ds(p0 + p, 1), :]
                sn = sin_ref[parity, z, pl.ds(p0 + p, 1), :]
                rows.append(
                    jnp.concatenate(
                        [
                            (vr * cs - vi * sn).astype(BF16),
                            (-(vr * sn + vi * cs)).astype(BF16),
                        ],
                        axis=1,
                    )
                )
            left = jnp.concatenate(rows, axis=0)
            real_rows, imag_rows = [], []
            for k in range(4):
                other = gamma_source[k][a] * 3 + c
                wr = modes_ref[z, other]
                wi = modes_ref[z, 12 + other]
                re, im = factor_parts[gamma_factor[k][a]]
                if re == 1:
                    gr, gi = wr, wi
                elif re == -1:
                    gr, gi = -wr, -wi
                elif im == 1:
                    gr, gi = -wi, wr
                else:
                    gr, gi = wi, -wr
                real_rows.append(jnp.concatenate([gr, -gi], axis=1))
                imag_rows.append(jnp.concatenate([gi, gr], axis=1))
            right = jnp.concatenate(real_rows + imag_rows, axis=0)
            total_ref[pl.ds(first, count * NMODE), :] += lax.dot_general(
                left, right, (((1,), (1,)), ((), ())), preferred_element_type=F32
            )


def plane_distance(step):
    dy, dx, dn, dc = step
    return -(min(dy, 4 - dy) + (2 * dx if not dn else 1)), -dc


plane_steps = sorted(
    [
        (dy, dx, dn, dc)
        for dy in range(4)
        for dx in range(2)
        for dn in range(2)
        for dc in range(2)
        if dy or dx or dn or dc
    ],
    key=plane_distance,
)
ring_steps = (4, 3, 5, 2, 6, 1, 7)


def kernel(
    nt, ns,
    e_hbm, links_hbm, clover_hbm, momenta_hbm, weights_hbm, sep_hbm,
    odd_ref, out_ref,
    e_ref, links_ref, clover_ref, momenta_ref, weights_ref, sep_ref,
    ef, ewide, e2, st, sz, ht, hz, tf, zf, lf, of, ob, cos_ref, sin_ref,
    total_ref, arr1, turn2, send2, arr2, gathered, send3, arr3,
    e_sem, in_sem, ts_sem, tr_sem, zs_sem, zr_sem, x_send, x_recv,
):
    t = lax.axis_index("ta")
    s = lax.axis_index("sa")
    tz, ty, tx = t // 8, lax.rem(t, 8) // 2, lax.rem(t, 2)
    t_up, t_dn = lax.rem(t + 1, nt), lax.rem(t + nt - 1, nt)
    s_up, s_dn = lax.rem(s + 1, ns), lax.rem(s + ns - 1, ns)
    partners = ((t_dn, s), (t_up, s), (t, s_dn), (t, s_up))
    place = lax.rem(t, 8) * 4 + s

    def in_plane(step):
        dy, dx, dn, dc = step
        x_half, x_near, core = lax.rem(tx + dx, 2), lax.rem(s // 2 + dn, 2), lax.rem(s + dc, 2)
        return tz * 8 + lax.rem(ty + dy, 4) * 2 + x_half, x_near * 2 + core

    def along_planes(step):
        return lax.rem(tz + step, 8) * 8 + lax.rem(t, 8), s

    loads = []
    e_loads = []
    for i in range(4):
        part = pl.ds(i * 384, 384)
        load = pltpu.make_async_copy(e_hbm.at[part], e_ref.at[part], e_sem.at[i])
        load.start()
        e_loads.append(load)
    for i, (source, target) in enumerate(
        (
            (momenta_hbm, momenta_ref), (links_hbm, links_ref), (clover_hbm, clover_ref),
            (weights_hbm, weights_ref), (sep_hbm, sep_ref),
        )
    ):
        load = pltpu.make_async_copy(source, target, in_sem.at[i])
        load.start()
        loads.append(load)
    barrier = pltpu.get_barrier_semaphore()
    for partner in partners[:2]:
        pl.semaphore_signal(barrier, inc=1, device_id=partner, device_id_type=MESH)
    plane_devices = [in_plane(step) for step in plane_steps]
    for device in plane_devices:
        pl.semaphore_signal(barrier, inc=1, device_id=device, device_id_type=MESH)
    for step in ring_steps:
        pl.semaphore_signal(barrier, inc=1, device_id=along_planes(step), device_id_type=MESH)

    for i, load in enumerate(e_loads):
        load.wait()
        part = pl.ds(i * 384, 384)
        ewide[part, :] = e_ref[part, :].astype(F32)
    sign_dn = jnp.where(t == 0, -1.0, 1.0).astype(F32)
    sign_up = jnp.where(t == nt - 1, -1.0, 1.0).astype(F32)

    def t_copy(way, z):
        return pltpu.make_async_remote_copy(
            src_ref=st.at[way, z],
            dst_ref=ht.at[way, z],
            send_sem=ts_sem.at[way, z],
            recv_sem=tr_sem.at[way, z],
            device_id=partners[way],
            device_id_type=MESH,
        )

    def z_copy(way):
        return pltpu.make_async_remote_copy(
            src_ref=sz.at[way],
            dst_ref=hz.at[way],
            send_sem=zs_sem.at[way],
            recv_sem=zr_sem.at[way],
            device_id=partners[2 + way],
            device_id_type=MESH,
        )

    def prepare(z):
        halves = []
        for g in range(2):
            halves.append(
                load_spin(
                    lambda comp: ewide[pl.ds((g * 8 * 24 + comp) * 4 + z, 8, stride=96), :]
                )
            )
        both = [
            [
                tuple(
                    jnp.concatenate([halves[0][a][c][q], halves[1][a][c][q]], axis=0)
                    for q in range(2)
                )
                for c in range(3)
            ]
            for a in range(4)
        ]
        for way, sign, factor in ((0, -1, sign_dn), (1, 1, sign_up)):
            half = project(both, 3, sign)
            for a in range(2):
                for c in range(3):
                    for q in range(2):
                        st[way, z, q * 6 + a * 3 + c] = (half[a][c][q] * factor).astype(BF16)
        for edge, way, sign in ((0, 0, -1), (ZL - 1, 1, 1)):
            if z == edge:
                half = project(both, 2, sign)
                for a in range(2):
                    for c in range(3):
                        for q in range(2):
                            sz[way, q * 6 + a * 3 + c] = half[a][c][q].astype(BF16)
        for a in range(4):
            for c in range(3):
                for q in range(2):
                    ef[z, q * 12 + a * 3 + c] = both[a][c][q]
                    e2[z, q * 12 + a * 3 + c] = both[a][c][q].astype(BF16)

    for z in (0, 3, 2, 1):
        prepare(z)
        if z == 0:
            pl.semaphore_wait(barrier, 2 + 31 + 7)
            z_copy(0).start()
        if z == ZL - 1:
            z_copy(1).start()
        for way in range(2):
            t_copy(way, z).start()

    loads[0].wait()
    phase_tables(t, s, momenta_ref[...], cos_ref, sin_ref)
    total_ref[...] = jnp.zeros_like(total_ref)

    def even_step(z, carry):
        meson_part(e2, 0, z, cos_ref, sin_ref, total_ref)
        return carry

    lax.fori_loop(0, ZL, even_step, 0)
    loads[1].wait()

    def widen_links(i, carry):
        rows = pl.ds(pl.multiple_of(i * 96, 96), 96)
        lf[rows, :] = links_ref[rows, :].astype(F32)
        return carry

    lax.fori_loop(0, 6, widen_links, 0)

    def z_halves(i, carry):
        z, g = i // 2, lax.rem(i, 2)
        rows = pl.ds(pl.multiple_of(g * 8, 8), 8)
        for way, sign, source, target in ((0, -1, z + 1, z), (1, 1, z, z + 1)):
            half = project(load_spin(lambda comp: ef[source, comp, rows, :]), 2, sign)
            for a in range(2):
                for c in range(3):
                    for q in range(2):
                        zf[way, target, q * 6 + a * 3 + c, rows, :] = half[a][c][q]
        return carry

    lax.fori_loop(0, 2 * (ZL - 1), z_halves, 0)
    for way in range(2):
        z_copy(way).wait_recv()
    zf[0, ZL - 1] = hz[0].astype(F32)
    zf[1, 0] = hz[1].astype(F32)
    lane = lax.broadcasted_iota(jnp.int32, (8, 128), 1)
    first, last = (lane & 7) == 0, (lane & 7) == 7

    def link(way, d, z):
        def load(q, a, b):
            row = ((((way * 4 + d) * 2 + q) * 3 + a) * 3 + b) * ZL
            return lf[pl.ds(row + z, 1), :]

        return load

    def stored(read):
        return [[(read(a * 3 + c), read(6 + a * 3 + c)) for c in range(3)] for a in range(2)]

    def near_step(i, carry):
        z, g = i // 2, lax.rem(i, 2)
        rows = pl.ds(pl.multiple_of(g * 8, 8), 8)
        shifted = ((t + s * ZL + z + (lane >> 3) + 1) & 1) == 1
        spin = load_spin(lambda comp: ef[z, comp, rows, :])
        zero = jnp.zeros((8, 128), F32)
        total = [[(zero, zero) for _ in range(3)] for _ in range(4)]

        def x_ahead(v):
            ahead = jnp.where(last, pltpu.roll(v, 7, 1), pltpu.roll(v, 127, 1))
            return jnp.where(shifted, ahead, v)

        def x_behind(v):
            behind = jnp.where(first, pltpu.roll(v, 121, 1), pltpu.roll(v, 1, 1))
            return jnp.where(shifted, v, behind)

        for way, sign in ((0, -1), (1, 1)):
            for d in range(3):
                if d == 0:
                    half = map_half(project(spin, 0, sign), (x_ahead, x_behind)[way])
                elif d == 1:
                    half = map_half(
                        project(spin, 1, sign), lambda v: pltpu.roll(v, (120, 8)[way], 1)
                    )
                else:
                    half = stored(lambda comp: zf[way, z, comp, rows, :])
                total = add_hop(total, link_times(link(way, d, z), half, way == 1), d, sign)
        for a in range(4):
            for c in range(3):
                for q in range(2):
                    of[z, q * 12 + a * 3 + c, rows, :] = total[a][c][q]
        return carry

    lax.fori_loop(0, 2 * ZL, near_step, 0)
    loads[2].wait()

    def far_hops(z):
        for way in range(2):
            t_copy(way, z).wait_recv()
            tf[way] = ht[way, z].astype(F32)

        def group_step(g, carry):
            rows = pl.ds(pl.multiple_of(g * 8, 8), 8)
            total = load_spin(lambda comp: of[z, comp, rows, :])
            for way, sign in ((0, -1), (1, 1)):
                half = stored(lambda comp: tf[way, comp, rows, :])
                total = add_hop(total, link_times(link(way, 3, z), half, way == 1), 3, sign)
            for chir in range(2):
                source = [
                    tuple(hop_kappa * total[2 * chir + col // 3][col % 3][q] for q in range(2))
                    for col in range(6)
                ]
                for r in range(6):
                    out_real = out_imag = None
                    for col in range(6):
                        row = ((chir * 2 * 6 + r) * 6 + col) * ZL
                        cr = clover_ref[pl.ds(row + z, 1), :]
                        ci = clover_ref[pl.ds(row + 36 * ZL + z, 1), :]
                        vr, vi = source[col]
                        re, im = cr * vr - ci * vi, cr * vi + ci * vr
                        out_real = re if out_real is None else out_real + re
                        out_imag = im if out_imag is None else out_imag + im
                    place = 6 * chir + r
                    of[z, place, rows, :] = out_real
                    of[z, 12 + place, rows, :] = out_imag
            return carry

        lax.fori_loop(0, 2, group_step, 0)
        ob[z] = of[z].astype(BF16)

    def far_step(i, carry):
        z = lax.rem(3 * i, ZL)
        far_hops(z)
        meson_part(ob, 1, z, cos_ref, sin_ref, total_ref)
        return carry

    lax.fori_loop(0, ZL - 1, far_step, 0)
    far_hops(1)

    def send(stage, source, target, slot, device):
        pltpu.make_async_remote_copy(
            src_ref=source,
            dst_ref=target.at[slot],
            send_sem=x_send.at[stage],
            recv_sem=x_recv.at[stage],
            device_id=device,
            device_id_type=MESH,
        ).start()

    def wait(stage, target, count, sems):
        others = target.at[pl.ds(0, count)]
        pltpu.make_async_copy(others, others, sems.at[stage]).wait()

    def rows_of(index):
        return pl.ds(pl.multiple_of(index * 8, 8), 8)

    pair = ty - 2 * (ty // 2)
    for half, rows in (
        (1 - ty // 2, (lax.rem(ty + 2, 4), lax.rem(ty + 2, 4) + 1 - 2 * pair)),
        (ty // 2, (ty + 1 - 2 * pair, ty)),
    ):
        meson_part(ob, 1, 1, cos_ref, sin_ref, total_ref, half * 8, 8)
        for y in rows:
            for dx, dn, dc in ((1, 0, 1), (1, 0, 0), (0, 1, 1), (0, 1, 0), (1, 1, 1), (1, 1, 0), (0, 0, 1), (0, 0, 0)):
                if y is ty and not (dx or dn or dc):
                    continue
                x_half, x_near, core = lax.rem(tx + dx, 2), lax.rem(s // 2 + dn, 2), lax.rem(s + dc, 2)
                device = (tz * 8 + y * 2 + x_half, x_near * 2 + core)
                send(0, total_ref.at[rows_of((y * 2 + x_half) * 4 + device[1])], arr1, place, device)
    arr1[place] = total_ref[rows_of(place), :]

    def turn(comp, carry):
        for z in range(ZL):
            for g in range(2):
                lf[pl.ds(g * 32 + z, 8, stride=4), :] = of[z, comp, pl.ds(g * 8, 8), :]
        odd_ref[:, comp] = lf[pl.ds(0, 64), :].astype(BF16).reshape(NMODE, ZL, 128)
        return carry

    lax.fori_loop(0, 24, turn, 0)
    loads[3].wait()
    loads[4].wait()
    weights = weights_ref[...]
    lane16 = lax.broadcasted_iota(jnp.int32, (NMODE, 128), 1)
    spread = (lane16 % NMODE == lax.broadcasted_iota(jnp.int32, (NMODE, 128), 0)).astype(F32)
    weight_j = jnp.dot(weights, spread, precision=lax.Precision.HIGHEST, preferred_element_type=F32)
    mode = lax.broadcasted_iota(jnp.int32, (1, NMODE), 1)
    pair_weights = [
        jnp.sum(
            jnp.where(mode == lax.rem(place, 2) * 8 + r, weights, 0.0), axis=1, keepdims=True
        )
        * weight_j
        for r in range(8)
    ]
    across = lax.broadcasted_iota(jnp.int32, (16, 16), 1)
    diagonal = across == lax.broadcasted_iota(jnp.int32, (16, 16), 0)
    separation = jnp.sum(
        jnp.where(diagonal, sep_ref[...].astype(F32), 0.0), axis=1, keepdims=True
    ).astype(jnp.int32)
    chosen = lax.broadcasted_iota(jnp.int32, (16, 128), 1) == lax.rem(t + separation, nt)
    for way in range(2):
        z_copy(way).wait_send()
        for z in range(ZL):
            t_copy(way, z).wait_send()
    wait(0, arr1, 31, x_recv)
    for j in range(8):
        field = arr1[4 * j] + arr1[4 * j + 1] + arr1[4 * j + 2] + arr1[4 * j + 3]
        turn2[pl.ds(j, 8, stride=8), :] = field
    send2[...] = turn2[pl.ds(0, 64), :].astype(BF16)
    for step in ring_steps:
        send(1, send2, arr2, tz, along_planes(step))
    arr2[tz] = send2[...]
    own = send2[...].astype(F32)
    weighted = [own[8 * r : 8 * r + 8] * pair_weights[r] for r in range(8)]
    high = [v.astype(BF16) for v in weighted]
    low = [(v - h.astype(F32)).astype(BF16) for v, h in zip(weighted, high)]
    sources = jnp.concatenate(
        [jnp.concatenate(high, axis=1), jnp.concatenate(low, axis=1)], axis=0
    )
    gathered[...] = jnp.zeros_like(gathered)
    wait(0, arr1, 31, x_send)
    wait(1, arr2, 7, x_recv)
    planes = [arr2[i].astype(F32) for i in range(8)]
    sinks = jnp.concatenate(
        [
            jnp.concatenate([planes[i][8 * r : 8 * r + 8] for i in range(8)], axis=0).astype(BF16)
            for r in range(8)
        ],
        axis=1,
    )
    product = lax.dot_general(
        sources, sinks, (((1,), (1,)), ((), ())), preferred_element_type=F32
    )
    gathered[:, :64] = product[:8] + product[8:]
    for j in range(8):
        send3[j] = gathered[pl.ds(j, 1), :]
    for device in plane_devices:
        send(2, send3.at[lax.rem(device[0], 8)], arr3, place, device)
    arr3[place] = send3[lax.rem(t, 8)]
    wait(1, arr2, 7, x_send)
    wait(2, arr3, 31, x_recv)
    row = jnp.sum(arr3[...], axis=0)
    picked = jnp.sum(jnp.where(chosen, row, 0.0), axis=1, keepdims=True)
    out_ref[...] = jnp.sum(jnp.where(diagonal, picked, 0.0), axis=0, keepdims=True) * (
        1.0 / (16.0 * NMODE * NMOM * LS**3)
    )
    wait(2, arr3, 31, x_send)


def finish_kernel(odd_ref, row_ref, odd_out, row_out, sems):
    copies = [
        pltpu.make_async_copy(odd_ref, odd_out, sems.at[0]),
        pltpu.make_async_copy(row_ref, row_out, sems.at[1]),
    ]
    for copy in copies:
        copy.start()
    for copy in copies:
        copy.wait()


def body(nt, ns, even_modes, hop_links, clover_inverse, momenta, mode_weights, separations):
    vmem = pl.BlockSpec(memory_space=pltpu.VMEM)
    hbm = pl.BlockSpec(memory_space=pltpu.HBM)
    shape = jax.ShapeDtypeStruct
    dma = pltpu.SemaphoreType.DMA
    sites = (ZL, 24, NMODE, 128)
    odd_modes, correlator = pl.pallas_call(
        functools.partial(kernel, nt, ns),
        out_shape=(pltpu.VMEM((NMODE, 24, ZL, 128), BF16), pltpu.VMEM((1, 16), F32)),
        in_specs=[hbm] * 6,
        out_specs=(vmem, vmem),
        scratch_shapes=[
            pltpu.VMEM((NMODE * 24 * ZL, 128), BF16),
            pltpu.VMEM((144 * ZL, 128), BF16),
            pltpu.VMEM((144 * ZL, 128), F32),
            pltpu.VMEM((3, NMOM), jnp.int32),
            pltpu.VMEM((1, NMODE), F32),
            pltpu.VMEM((1, 16), jnp.int32),
            pltpu.VMEM(sites, F32),
            pltpu.VMEM(((NMODE + 1) * 24 * ZL, 128), F32),
            pltpu.VMEM(sites, BF16),
            pltpu.VMEM((2, ZL, 12, NMODE, 128), BF16),
            pltpu.VMEM((2, 12, NMODE, 128), BF16),
            pltpu.VMEM((2, ZL, 12, NMODE, 128), BF16),
            pltpu.VMEM((2, 12, NMODE, 128), BF16),
            pltpu.VMEM((2, 12, NMODE, 128), F32),
            pltpu.VMEM((2, ZL, 12, NMODE, 128), F32),
            pltpu.VMEM((144 * ZL, 128), F32),
            pltpu.VMEM(sites, F32),
            pltpu.VMEM(sites, BF16),
            pltpu.VMEM((2, ZL, NMOM, 128), F32),
            pltpu.VMEM((2, ZL, NMOM, 128), F32),
            pltpu.VMEM((NMOM * NMODE, 128), F32),
            pltpu.VMEM((32, 8, 128), F32),
            pltpu.VMEM((72, 128), F32),
            pltpu.VMEM((64, 128), BF16),
            pltpu.VMEM((8, 64, 128), BF16),
            pltpu.VMEM((8, 128), F32),
            pltpu.VMEM((8, 1, 128), F32),
            pltpu.VMEM((32, 1, 128), F32),
            dma((4,)), dma((5,)), dma((2, ZL)), dma((2, ZL)), dma((2,)), dma((2,)), dma((3,)), dma((3,)),
        ],
        compiler_params=pltpu.CompilerParams(
            collective_id=0, has_side_effects=True, vmem_limit_bytes=63 * 1024 * 1024
        ),
        name="correlator",
    )(
        even_modes.reshape(NMODE * 24 * ZL, 128),
        hop_links.reshape(144 * ZL, 128),
        clover_inverse.reshape(144 * ZL, 128),
        momenta.T,
        mode_weights.reshape(1, NMODE),
        separations,
    )
    odd_modes, correlator = pl.pallas_call(
        finish_kernel,
        out_shape=(shape(odd_modes.shape, BF16), shape((1, 16), F32)),
        in_specs=[vmem, vmem],
        out_specs=(hbm, hbm),
        scratch_shapes=[dma((2,))],
        compiler_params=pltpu.CompilerParams(vmem_limit_bytes=1024 * 1024),
        name="finish",
    )(odd_modes, correlator)
    return odd_modes.reshape(even_modes.shape), correlator


def solution(mesh):
    in_specs = (
        P(None, None, None, None, "ta", "sa", None),
        P(None, None, None, None, None, "ta", "sa", None),
        P(None, None, None, None, "ta", "sa", None),
        P(),
        P(),
        P("ta", None),
    )
    out_specs = (P(None, None, None, None, "ta", "sa", None), P("ta", None))
    return jax.shard_map(
        functools.partial(body, mesh.shape["ta"], mesh.shape["sa"]),
        mesh=mesh,
        in_specs=in_specs,
        out_specs=out_specs,
        check_vma=False,
    )
```
